512 devices in a mesh: space: 8 (over y, x_lo), filt: 64 (over x_hi, z, core).
Axes of the slice: x: 4 (x_hi: 2, x_lo: 2; x = x_hi * 2 + x_lo), y: 4, z: 16, core: 2. Of those that a mesh axis runs over, the one named last changes fastest.
Arguments:
- quantized: bfloat16 [256, 8, 128, 128], P('filt', 'space'), may hold values from -6 to 6
- scales: float32 [256, 8], P('filt', 'space'), may hold values from 0.3 to 3
- weights: bfloat16 [256, 27, 256], P('filt'), may hold values from -0.078125 to 0.078125
- cotangent: bfloat16 [256, 8, 128, 128], P('filt', 'space'), may hold values from -6 to 6
Outputs:
- output: bfloat16 [256, 8, 128, 128], P('filt', 'space')
- input_grad: bfloat16 [256, 8, 128, 128], P('filt', 'space')
- weight_grad: float32 [256, 27, 256], P('filt')
The draws below stay inside these ranges and needn't reach their ends.
All inputs are finite; a program needn't handle non-finite values.
Results may differ from the reference program's by a relative error of at most 0.0049.
Values may be sent and summed in bfloat16 or wider, within the bound.
No kernel may reach another device: no remote copies, remote signals or barrier semaphores. Data moves between devices by JAX's collectives and lax.ppermute only.
A program may use at most 64 MiB of HBM per device.

```python
import math
import jax
import jax.numpy as jnp
from jax import lax

CIN = 256
COUT = 256
HY = 128
WX = 128
NZ = 8


def steps_of(own_key, dims, pieces, least, high):
    factor_of = 1.0
    for axis_at, shards_of in pieces:
        draws = jax.random.uniform(jax.random.fold_in(jax.random.fold_in(own_key, 6), axis_at), (shards_of,), jnp.float32, least / len(pieces), high / len(pieces))
        factor_of = factor_of * jnp.repeat(jnp.exp(draws), dims[axis_at] // shards_of).reshape((-1,) + (1,) * (len(dims) - 1 - axis_at))
    return factor_of


def bell_draw(stream_key, extent, spread, limit, cuts=(), kind=jnp.bfloat16):
    values = spread * jax.random.normal(stream_key, extent, jnp.float32)
    if cuts:
        values = values * steps_of(stream_key, extent, cuts, -0.22, 0.18)
    return jnp.clip(values, -limit, limit).astype(kind)


def setup_inputs(seed: int = 0) -> dict:
    splits = jax.random.split(jax.random.key(seed), 5)
    quantized = bell_draw(splits[0], (CIN, NZ, HY, WX), 1.0, 6.0, ((0, 64), (1, 8)))
    scales = jnp.clip(jnp.exp(math.log(3.0) - 2.3025851 * jax.random.uniform(splits[1], (CIN, NZ), jnp.float32) ** steps_of(splits[1], (CIN, NZ), ((0, 64), (1, 8)), -0.2, 0.2)), 0.3, 3.0)
    weights = bell_draw(splits[2], (CIN, 27, COUT), (27 * CIN) ** -0.5, 0.078125, ((0, 64),))
    cotangent = bell_draw(splits[3], (COUT, NZ, HY, WX), 1.0, 6.0, ((0, 64), (1, 8)))
    return {"quantized": quantized, "scales": scales, "weights": weights, "cotangent": cotangent}


def convolve(volume, kernel_full):
    return lax.conv_general_dilated(volume[None], kernel_full, (1, 1, 1), 'SAME', dimension_numbers=('NCDHW', 'OIDHW', 'NCDHW'), precision=lax.Precision.HIGHEST)[0]

def reference(quantized, scales, weights, cotangent):
    dequant = (quantized.astype(jnp.float32) * scales[:, :, None, None]).astype(jnp.bfloat16)
    dequant = lax.optimization_barrier(dequant)
    kernel_full = weights.astype(jnp.float32).reshape(CIN, 3, 3, 3, COUT).transpose(4, 0, 1, 2, 3)
    output, pullback = jax.vjp(convolve, dequant.astype(jnp.float32), kernel_full)
    input_grad, kernel_grad = pullback(cotangent.astype(jnp.float32))
    grad_norm = 1.0 / math.sqrt(NZ * HY * WX)
    weight_grad = kernel_grad.transpose(1, 2, 3, 4, 0).reshape(CIN, 27, COUT) * grad_norm
    return (output.astype(jnp.bfloat16), input_grad.astype(jnp.bfloat16), weight_grad.astype(jnp.float32))
```

```python
import math

import jax
import jax.numpy as jnp
from jax import lax
from jax.experimental import pallas as pl
from jax.experimental.pallas import tpu as pltpu
from jax.sharding import PartitionSpec as P


F32 = jnp.float32
BF16 = jnp.bfloat16
PARAMS = pltpu.CompilerParams(vmem_limit_bytes=32 * 1024 * 1024)


def select_rows(rows, source, columns):
    row = lax.broadcasted_iota(jnp.int32, (rows, columns), 0)
    col = lax.broadcasted_iota(jnp.int32, (rows, columns), 1)
    return jnp.where(source(row) == col, 1.0, 0.0).astype(BF16)


def moved(matrix, cells):
    return jnp.dot(matrix, cells, preferred_element_type=F32).astype(BF16)


def y_first(n):
    return ((n >> 1) & 31) * 8 + (n & 1) * 4 + (n >> 6)


def y_last(n):
    return (n & 3) * 64 + (n >> 3) * 2 + ((n >> 2) & 1)


def j_first(n):
    return (n & 1) * 128 + ((n >> 1) & 15) * 8 + (n >> 5)


def j_last(n):
    return (n & 7) * 32 + ((n >> 3) & 15) * 2 + (n >> 7)


def rim_first(n):
    return ((n >> 4) & 1) * 128 + ((n >> 1) & 7) * 16 + (n & 1) * 8 + (n >> 5) + 1


def rim_last(n):
    return jnp.where(((n & 7) >= 1) & ((n & 7) <= 6), ((n & 7) - 1) * 16 + (n >> 3), -1)


def forward_kernel(half_ref, cells_ref, mine_ref, theirs_ref, keep_ref, send_ref, dequant_ref, filter_ref, planes):
    first = half_ref[0] == 0
    by_j = select_rows(256, j_first, 256)
    for block in range(4):
        part = pl.ds(block * 128, 128)
        mine, theirs = mine_ref[part], theirs_ref[part]
        pair = jnp.concatenate([jnp.where(first, mine, theirs), jnp.where(first, theirs, mine)], axis=0)
        lanes = moved(by_j, pair)
        for j in range(7):
            filter_ref[block * 32 : block * 32 + 32, j * 128 : j * 128 + 128] = lanes[j * 32 : j * 32 + 32]
    turned = jnp.concatenate([filter_ref[:, j * 128 : j * 128 + 128].T for j in range(7)], axis=0)
    stacked = jnp.concatenate([turned[a * 288 : a * 288 + 288] for a in range(3)], axis=1)

    by_y = select_rows(256, y_first, 256)
    planes[0] = jnp.zeros((128, 512), BF16)
    planes[9] = jnp.zeros((128, 512), BF16)

    def arrange(z, _):
        for part in range(2):
            rows = moved(by_y, cells_ref[z, part * 256 : part * 256 + 256])
            for y in range(4):
                piece = rows[y * 64 : y * 64 + 64]
                planes[z + 1, part * 64 : part * 64 + 64, y * 128 : y * 128 + 128] = piece
                dequant_ref[z, part * 64 : part * 64 + 64, y * 128 : y * 128 + 128] = piece
        return 0

    lax.fori_loop(0, 8, arrange, 0)
    column = lax.broadcasted_iota(jnp.int32, (32, 128), 1)

    def plane(z, _):
        near = jnp.concatenate([planes[z], planes[z + 1], planes[z + 2]], axis=0)
        terms = jnp.dot(stacked, near, preferred_element_type=F32)
        for row in range(6):
            sums = []
            for e in range(3):
                total = None
                for b in range(3):
                    y = row + b - 2
                    if 0 <= y < 4:
                        at = b * 96 + e * 32
                        term = terms[at : at + 32, y * 128 : y * 128 + 128]
                        total = term if total is None else total + term
                sums.append(total)
            left = jnp.where(column >= 1, pltpu.roll(sums[0], 1, 1), 0.0)
            right = jnp.where(column <= 126, pltpu.roll(sums[2], 127, 1), 0.0)
            result = sums[1] + left + right
            keep_ref[z, row] = result[:16]
            send_ref[z, row] = result[16:]
        return 0

    lax.fori_loop(0, 8, plane, 0)


def backward_kernel(mine_ref, theirs_ref, dequant_ref, filter_ref, grad_ref, filter_grad_ref, shifted, image, total):
    by_rim = select_rows(192, rim_first, 256)
    before = select_rows(128, lambda n: n - 1, 128)
    after = select_rows(128, lambda n: n + 1, 128)
    shifted[0] = jnp.zeros((96, 768), BF16)
    shifted[9] = jnp.zeros((96, 768), BF16)
    image[864:896] = jnp.zeros((32, 512), BF16)
    total[...] = jnp.zeros((128, 896), F32)

    def arrange(z, _):
        rows = moved(by_rim, jnp.concatenate([mine_ref[z], theirs_ref[z]], axis=0))
        for e, cells in ((0, moved(rows, before)), (1, rows), (2, moved(rows, after))):
            for y in range(6):
                shifted[z + 1, e * 32 : e * 32 + 32, y * 128 : y * 128 + 128] = cells[y * 32 : y * 32 + 32]
        return 0

    lax.fori_loop(0, 8, arrange, 0)
    back_y = select_rows(256, y_last, 256)

    def plane(z, _):
        for a in range(3):
            for b in range(3):
                at = (a * 3 + b) * 96
                image[at : at + 96] = shifted[z + 2 - a, :, (2 - b) * 128 : (2 - b) * 128 + 512]
        grad = jnp.dot(filter_ref[...], image[...], preferred_element_type=F32).astype(BF16)
        for part in range(2):
            rows = jnp.concatenate(
                [grad[part * 64 : part * 64 + 64, y * 128 : y * 128 + 128] for y in range(4)], axis=0
            )
            grad_ref[z, part * 256 : part * 256 + 256] = moved(back_y, rows)
        total[...] += lax.dot_general(
            dequant_ref[z], image[...], (((1,), (1,)), ((), ())), preferred_element_type=F32
        )
        return 0

    lax.fori_loop(0, 8, plane, 0)
    back_j = select_rows(256, j_last, 256)
    for block in range(4):
        rows = [total[block * 32 : block * 32 + 32, j * 128 : j * 128 + 128].astype(BF16) for j in range(7)]
        rows = moved(back_j, jnp.concatenate(rows + [jnp.zeros((32, 128), BF16)], axis=0))
        filter_grad_ref[0, block * 128 : block * 128 + 128] = rows[:128]
        filter_grad_ref[1, block * 128 : block * 128 + 128] = rows[128:]


def sum_kernel(keep_ref, other_ref, out_ref):
    back_rim = select_rows(128, rim_last, 96)
    for z in range(8):
        rows = (keep_ref[z] + other_ref[z]).astype(BF16).reshape(96, 128)
        out_ref[z] = moved(back_rim, rows)


def windows(rows):
    lead = rows.shape[:-2]
    padded = jnp.pad(rows, [(0, 0)] * len(lead) + [(2, 2), (0, 0)]).reshape(lead + (33, 4, 128))
    return jnp.concatenate([padded[..., :32, :, :], padded[..., 1:, :, :]], axis=-2)


def overlapped(parts):
    lead = parts.shape[:-3]
    keep = [(0, 0)] * len(lead)
    first = jnp.pad(parts[..., :4, :], keep + [(0, 1), (0, 0), (0, 0)])
    second = jnp.pad(parts[..., 4:, :], keep + [(1, 0), (0, 0), (0, 0)])
    return (first + second).reshape(lead + (132, 128))[..., 2:130, :]


def local(quantized, scales, weights, cotangent):
    rank = lax.axis_index("filt")
    slab = lax.axis_index("space")
    x_hi = rank // 32
    swap_core = [(n, n ^ 1) for n in range(64)]
    swap_x = [(n, n ^ 32) for n in range(64)]

    dequant = (quantized.astype(F32) * scales[:, :, None, None]).astype(BF16)
    cells = dequant.reshape(2, 2, 32, 4, 128).transpose(2, 0, 1, 3, 4).reshape(64, 8, 128)
    rims = windows(cotangent.reshape(2, 2, 128, 128)).transpose(2, 0, 1, 3, 4).reshape(64, 16, 128)
    own = lax.dynamic_slice_in_dim(weights, slab * 32, 32, axis=2).reshape(2, 2, 27, 8, 2, 2)
    own = own.transpose(0, 1, 2, 4, 3, 5)
    own = jnp.stack([own[0], own[1][:, :, ::-1]], axis=1).reshape(2, 2, 864)
    own = jnp.pad(own, ((0, 0), (0, 0), (0, 160))).reshape(2, 1, 2, 8, 128)
    own = jnp.broadcast_to(own, (2, 16, 2, 8, 128)).reshape(64, 8, 128)
    got = lax.all_to_all(jnp.concatenate([cells, rims, own], axis=1), "filt", 0, 0, tiled=True)

    filters = got[:, 24:].reshape(512, 128)
    other_filters = lax.ppermute(filters, "filt", swap_x)
    cells = jnp.broadcast_to(got[:, :8].reshape(1, 512, 128), (8, 512, 128))
    rims = got[:, 8:24].reshape(8, 128, 128)
    got = lax.all_to_all(jnp.concatenate([cells, rims], axis=1), "space", 0, 0, tiled=True)
    other_rims = lax.ppermute(got[:, 512:], "filt", swap_core)

    keep, send, cells, filters = pl.pallas_call(
        forward_kernel,
        grid=(1,),
        out_shape=(
            jax.ShapeDtypeStruct((8, 6, 16, 128), F32),
            jax.ShapeDtypeStruct((8, 6, 16, 128), F32),
            jax.ShapeDtypeStruct((8, 128, 512), BF16),
            jax.ShapeDtypeStruct((128, 896), BF16),
        ),
        in_specs=[
            pl.BlockSpec(memory_space=pltpu.SMEM),
            pl.BlockSpec((8, 512, 128), lambda n: (0, 0, 0)),
            pl.BlockSpec((512, 128), lambda n: (0, 0)),
            pl.BlockSpec((512, 128), lambda n: (0, 0)),
        ],
        out_specs=(
            pl.BlockSpec((8, 6, 16, 128), lambda n: (0, 0, 0, 0)),
            pl.BlockSpec((8, 6, 16, 128), lambda n: (0, 0, 0, 0)),
            pl.BlockSpec((8, 128, 512), lambda n: (0, 0, 0)),
            pl.BlockSpec((128, 896), lambda n: (0, 0)),
        ),
        scratch_shapes=[pltpu.VMEM((10, 128, 512), BF16)],
        compiler_params=PARAMS,
        cost_estimate=pl.CostEstimate(flops=2 * 8 * 288 * 384 * 512, bytes_accessed=4 << 20, transcendentals=0),
        name="forward",
    )(x_hi.reshape(1).astype(jnp.int32), got, filters, other_filters)
    other = lax.ppermute(send, "filt", swap_core)

    grad, filter_grad = pl.pallas_call(
        backward_kernel,
        grid=(1,),
        out_shape=(
            jax.ShapeDtypeStruct((8, 512, 128), BF16),
            jax.ShapeDtypeStruct((2, 512, 128), BF16),
        ),
        in_specs=[
            pl.BlockSpec((8, 128, 128), lambda n: (0, 4, 0)),
            pl.BlockSpec((8, 128, 128), lambda n: (0, 0, 0)),
            pl.BlockSpec((8, 128, 512), lambda n: (0, 0, 0)),
            pl.BlockSpec((128, 896), lambda n: (0, 0)),
        ],
        out_specs=(
            pl.BlockSpec((8, 512, 128), lambda n: (0, 0, 0)),
            pl.BlockSpec((2, 512, 128), lambda n: (0, 0, 0)),
        ),
        scratch_shapes=[
            pltpu.VMEM((10, 96, 768), BF16),
            pltpu.VMEM((896, 512), BF16),
            pltpu.VMEM((128, 896), F32),
        ],
        compiler_params=PARAMS,
        cost_estimate=pl.CostEstimate(flops=4 * 8 * 896 * 128 * 512, bytes_accessed=4 << 20, transcendentals=0),
        name="backward",
    )(got, other_rims, cells, filters)

    filter_keep = jnp.where(x_hi == 0, filter_grad[0], filter_grad[1])
    filter_send = jnp.where(x_hi == 0, filter_grad[1], filter_grad[0])
    filter_other = lax.ppermute(filter_send, "filt", swap_x)

    out = pl.pallas_call(
        sum_kernel,
        out_shape=jax.ShapeDtypeStruct((8, 128, 128), BF16),
        compiler_params=PARAMS,
        name="sum",
    )(keep, other)

    got = lax.all_to_all(jnp.concatenate([grad, out], axis=1), "space", 0, 0, tiled=True)
    grad = jnp.sum(got[:, :512].astype(F32), axis=0).astype(BF16).reshape(64, 8, 128)
    out = got[:, 512:].reshape(64, 16, 128)
    filter_grad = (filter_keep.astype(F32) + filter_other.astype(F32)).astype(BF16).reshape(64, 8, 128)
    got = lax.all_to_all(jnp.concatenate([grad, out, filter_grad], axis=1), "filt", 0, 0, tiled=True)

    got = got.reshape(32, 2, 32, 128)
    grad = got[:, :, :8].reshape(32, 2, 2, 4, 128).transpose(1, 2, 0, 3, 4).reshape(4, 1, 128, 128)
    out = got[:, :, 8:24].reshape(32, 2, 2, 8, 128).transpose(1, 2, 0, 3, 4).astype(F32)
    out = overlapped(out).astype(BF16).reshape(4, 1, 128, 128)

    norm = 1.0 / math.sqrt(131072)
    summed = jnp.sum(got[:, :, 24:].reshape(2, 16, 2, 8, 128).astype(F32), axis=1) * norm
    summed = summed.transpose(1, 0, 2, 3).reshape(1, 32, 128)
    gathered = lax.all_to_all(jnp.broadcast_to(summed, (8, 32, 128)), "space", 0, 0, tiled=True)
    gathered = gathered.reshape(8, 2, 2, 1024)[..., :864].reshape(8, 2, 2, 27, 2, 8, 2)
    gathered = jnp.stack([gathered[:, 0], gathered[:, 1][:, :, :, ::-1]], axis=1)
    filter_grad = gathered.transpose(1, 2, 3, 0, 5, 4, 6).reshape(4, 27, 256)
    return (out, grad, filter_grad)


def solution(mesh):
    placed = (
        P("filt", "space", None, None),
        P("filt", "space"),
        P("filt", None, None),
        P("filt", "space", None, None),
    )
    return jax.shard_map(
        local,
        mesh=mesh,
        in_specs=placed,
        out_specs=(
            P("filt", "space", None, None),
            P("filt", "space", None, None),
            P("filt", None, None),
        ),
        check_vma=False,
    )
```

```python
import math

import jax
import jax.numpy as jnp
from jax import lax
from jax.experimental import pallas as pl
from jax.experimental.pallas import tpu as pltpu
from jax.sharding import PartitionSpec as P


F32 = jnp.float32
BF16 = jnp.bfloat16
PARAMS = pltpu.CompilerParams(vmem_limit_bytes=32 * 1024 * 1024)
UNROLL = 2


def select_rows(rows, source, columns):
    row = lax.broadcasted_iota(jnp.int32, (rows, columns), 0)
    col = lax.broadcasted_iota(jnp.int32, (rows, columns), 1)
    return jnp.where(source(row) == col, 1.0, 0.0).astype(BF16)


def moved(matrix, cells):
    return jnp.dot(matrix, cells, preferred_element_type=F32).astype(BF16)


def y_first(n):
    return ((n >> 1) & 31) * 8 + (n & 1) * 4 + (n >> 6)


def y_last(n):
    return (n & 3) * 64 + (n >> 3) * 2 + ((n >> 2) & 1)


def n_first(n):
    return (n & 1) * 128 + ((n >> 1) & 31) * 4 + (n >> 6)


def n_last(n):
    return (n & 3) * 64 + ((n >> 2) & 31) * 2 + (n >> 7)


def rim_first(core):
    return lambda n: (((n >> 1) & 1) ^ core) * 128 + ((n >> 2) & 7) * 16 + (n & 1) * 8 + (n >> 5) + 1


def rim_last(n):
    return jnp.where(((n & 7) >= 1) & ((n & 7) <= 6), ((n & 7) - 1) * 16 + (n >> 3), -1)


def own_first(core):
    return lambda n: (n & 96) + ((n >> 1) & 7) * 4 + (((n >> 4) & 1) ^ core) * 2 + (n & 1)


def slot(rank, quarter):
    x = ((rank >> 1) & 3) ^ quarter
    return ((x & 1) << 1) | (x >> 1)


def forward_kernel(rank_ref, cells_ref, slots_ref, keep_ref, send_ref, planes_ref, filter_ref):
    rank = rank_ref[0]
    by_n = select_rows(256, n_first, 256)
    for h in range(2):
        for part in range(2):
            pair = [slots_ref[slot(rank, 2 * i + h), part * 128 : part * 128 + 128] for i in range(2)]
            lanes = moved(by_n, jnp.concatenate(pair, axis=0))
            for n in range(4 - h):
                at = (4 * h + n) * 128
                filter_ref[part * 64 : part * 64 + 64, at : at + 128] = lanes[n * 64 : n * 64 + 64]
    order = select_rows(128, own_first(rank & 1), 128)
    turned = [
        lax.dot_general(
            order,
            filter_ref[:, j * 128 : j * 128 + 128],
            (((1,), (1,)), ((), ())),
            preferred_element_type=F32,
        ).astype(BF16)
        for j in range(7)
    ]
    turned = jnp.concatenate(turned, axis=0)
    stacked = jnp.concatenate([turned[a * 288 : a * 288 + 288] for a in range(3)], axis=1)

    by_y = select_rows(256, y_first, 256)
    planes_ref[0] = jnp.zeros((128, 512), BF16)
    planes_ref[9] = jnp.zeros((128, 512), BF16)

    def arrange(z, _):
        for part in range(2):
            rows = moved(by_y, cells_ref[z, part * 256 : part * 256 + 256])
            for y in range(4):
                piece = rows[y * 64 : y * 64 + 64]
                planes_ref[z + 1, part * 64 : part * 64 + 64, y * 128 : y * 128 + 128] = piece
        return 0

    lax.fori_loop(0, 8, arrange, 0, unroll=UNROLL)
    column = lax.broadcasted_iota(jnp.int32, (32, 128), 1)

    def plane(z, _):
        near = jnp.concatenate([planes_ref[z], planes_ref[z + 1], planes_ref[z + 2]], axis=0)
        terms = jnp.dot(stacked, near, preferred_element_type=F32)
        for row in range(6):
            sums = []
            for e in range(3):
                total = None
                for b in range(3):
                    y = row + b - 2
                    if 0 <= y < 4:
                        at = b * 96 + e * 32
                        term = terms[at : at + 32, y * 128 : y * 128 + 128]
                        total = term if total is None else total + term
                sums.append(total)
            left = jnp.where(column >= 1, pltpu.roll(sums[0], 1, 1), 0.0)
            right = jnp.where(column <= 126, pltpu.roll(sums[2], 127, 1), 0.0)
            result = sums[1] + left + right
            keep_ref[z, row] = result[:16]
            send_ref[z, row] = result[16:]
        return 0

    lax.fori_loop(0, 8, plane, 0, unroll=UNROLL)


def fill_image(image, shifted_ref, z):
    for a in range(3):
        for b in range(3):
            at = (a * 3 + b) * 96
            image[at : at + 96] = shifted_ref[z + 2 - a, :, (2 - b) * 128 : (2 - b) * 128 + 512]


def backward_kernel(rank_ref, mine_ref, theirs_ref, filter_ref, grad_ref, shifted_ref, image):
    by_rim = select_rows(192, rim_first(rank_ref[0] & 1), 256)
    before = select_rows(128, lambda n: n - 1, 128)
    after = select_rows(128, lambda n: n + 1, 128)
    shifted_ref[0] = jnp.zeros((96, 768), BF16)
    shifted_ref[9] = jnp.zeros((96, 768), BF16)
    image[864:896] = jnp.zeros((32, 512), BF16)

    def arrange(z, _):
        rows = moved(by_rim, jnp.concatenate([mine_ref[z], theirs_ref[z]], axis=0))
        for e, cells in ((0, moved(rows, before)), (1, rows), (2, moved(rows, after))):
            for y in range(6):
                shifted_ref[z + 1, e * 32 : e * 32 + 32, y * 128 : y * 128 + 128] = cells[y * 32 : y * 32 + 32]
        return 0

    lax.fori_loop(0, 8, arrange, 0, unroll=UNROLL)
    back_y = select_rows(256, y_last, 256)

    def plane(z, _):
        fill_image(image, shifted_ref, z)
        grad = jnp.dot(filter_ref[...], image[...], preferred_element_type=F32).astype(BF16)
        for part in range(2):
            rows = jnp.concatenate(
                [grad[part * 64 : part * 64 + 64, y * 128 : y * 128 + 128] for y in range(4)], axis=0
            )
            grad_ref[z, part * 256 : part * 256 + 256] = moved(back_y, rows)
        return 0

    lax.fori_loop(0, 8, plane, 0, unroll=UNROLL)


def filter_grad_kernel(rank_ref, planes_ref, shifted_ref, slots_ref, image, total):
    image[864:896] = jnp.zeros((32, 512), BF16)
    total[...] = jnp.zeros((128, 896), F32)

    def plane(z, _):
        fill_image(image, shifted_ref, z)
        total[...] += lax.dot_general(
            planes_ref[z + 1], image[...], (((1,), (1,)), ((), ())), preferred_element_type=F32
        )
        return 0

    lax.fori_loop(0, 8, plane, 0, unroll=UNROLL)
    back_n = select_rows(256, n_last, 256)
    for h in range(2):
        for part in range(2):
            rows = [
                total[part * 64 : part * 64 + 64, j * 128 : j * 128 + 128].astype(BF16)
                if j < 7
                else jnp.zeros((64, 128), BF16)
                for j in range(4 * h, 4 * h + 4)
            ]
            rows = moved(back_n, jnp.concatenate(rows, axis=0))
            for i in range(2):
                place = slot(rank_ref[0], 2 * i + h)
                slots_ref[place, part * 128 : part * 128 + 128] = rows[i * 128 : i * 128 + 128]


def sum_kernel(keep_ref, other_ref, out_ref):
    back_rim = select_rows(128, rim_last, 96)
    for z in range(8):
        rows = (keep_ref[z] + other_ref[z]).astype(BF16).reshape(96, 128)
        out_ref[z] = moved(back_rim, rows)


def finish_kernel(parts_ref, out_ref, by_tap):
    column = lax.broadcasted_iota(jnp.int32, (8, 128), 1) // 32
    norm = 1.0 / math.sqrt(131072)
    for channel in range(4):
        for half in range(2):
            parts = [parts_ref[half * 4 + n, channel] for n in range(4)]
            for tap in range(4):
                rows = jnp.zeros((8, 128), F32)
                for n in range(4):
                    turned = parts[n] if n == tap else pltpu.roll(parts[n], (n - tap) % 4 * 32, 1)
                    rows = jnp.where(column == n, turned, rows)
                by_tap[channel * 2 + half, pl.ds(tap, 8, stride=4)] = rows * norm
            out_ref[channel, :, half * 128 : half * 128 + 128] = by_tap[channel * 2 + half, :27]


def windows(rows):
    lead = rows.shape[:-2]
    padded = jnp.pad(rows, [(0, 0)] * len(lead) + [(2, 2), (0, 0)]).reshape(lead + (33, 4, 128))
    return jnp.concatenate([padded[..., :32, :, :], padded[..., 1:, :, :]], axis=-2)


def overlapped(parts):
    lead = parts.shape[:-3]
    keep = [(0, 0)] * len(lead)
    first = jnp.pad(parts[..., 1:4, :], keep + [(0, 1), (1, 0), (0, 0)])
    second = jnp.pad(parts[..., 4:7, :], keep + [(1, 0), (0, 1), (0, 0)])
    return (first + second).reshape(lead + (132, 128))[..., 2:130, :]


def with_corners(rims, rows):
    return jnp.concatenate([rows[..., :1, :], rims[..., 1:7, :], rows[..., 1:, :]], axis=-2)


def corners(rims):
    return jnp.concatenate([rims[..., :1, :], rims[..., 7:, :]], axis=-2)


def whole(*shape):
    return pl.BlockSpec(shape, lambda n: (0,) * len(shape))


SCALAR = pl.BlockSpec(memory_space=pltpu.SMEM)


def call(kernel, name, ins, outs, scratch, flops):
    return pl.pallas_call(
        kernel,
        grid=(1,),
        in_specs=ins,
        out_shape=[jax.ShapeDtypeStruct(shape, dtype) for shape, dtype in outs],
        out_specs=[whole(*shape) for shape, _ in outs],
        scratch_shapes=[pltpu.VMEM(shape, dtype) for shape, dtype in scratch],
        compiler_params=PARAMS,
        cost_estimate=pl.CostEstimate(flops=flops, bytes_accessed=4 << 20, transcendentals=0),
        name=name,
    )


def swapped(array, axis, bit):
    count = lax.axis_size(axis)
    return lax.ppermute(array, axis, [(n, n ^ bit) for n in range(count)])


def local(quantized, scales, weights, cotangent):
    rank = lax.axis_index("filt").reshape(1).astype(jnp.int32)
    slab = lax.axis_index("space").reshape(1).astype(jnp.int32)

    dequant = (quantized.astype(F32) * scales[:, :, None, None]).astype(BF16)
    cells = dequant.reshape(2, 2, 32, 4, 128).transpose(2, 0, 1, 3, 4).reshape(64, 8, 128)
    rims = windows(cotangent.reshape(2, 2, 128, 128)).transpose(2, 0, 1, 3, 4).reshape(8, 4, 2, 2, 8, 128)
    own = lax.dynamic_slice_in_dim(weights, slab[0] * 32, 32, axis=2).reshape(4, 864)
    own = jnp.pad(own, ((0, 0), (0, 160))).reshape(2, 4, 2, 2, 128).transpose(1, 0, 2, 3, 4)
    own = jnp.broadcast_to(own[None], (8, 4, 2, 2, 2, 128))
    rims = with_corners(rims, own).reshape(64, 16, 128)
    got = lax.all_to_all(jnp.concatenate([cells, rims], axis=1), "filt", 0, 0, tiled=True)

    filters = corners(got[:, 8:24].reshape(64, 2, 8, 128)).reshape(1, 256, 128)
    for bit in (4, 2):
        filters = jnp.concatenate([filters, swapped(filters, "filt", bit)], axis=0)

    cells = jnp.broadcast_to(got[:, :8].reshape(1, 512, 128), (8, 512, 128))
    rims = got[:, 8:24].reshape(8, 128, 128)
    got = lax.all_to_all(jnp.concatenate([cells, rims], axis=1), "space", 0, 0, tiled=True)
    other_rims = swapped(got[:, 512:], "filt", 1)

    keep, send, planes, filters = call(
        forward_kernel,
        "forward",
        [SCALAR, whole(8, 512, 128), whole(4, 256, 128)],
        [((8, 6, 16, 128), F32), ((8, 6, 16, 128), F32), ((10, 128, 512), BF16), ((128, 896), BF16)],
        [],
        2 * 8 * 288 * 384 * 512,
    )(rank, got, filters)
    other = swapped(send, "filt", 1)
    grad, shifted = call(
        backward_kernel,
        "backward",
        [SCALAR, pl.BlockSpec((8, 128, 128), lambda n: (0, 4, 0)), whole(8, 128, 128), whole(128, 896)],
        [((8, 512, 128), BF16), ((10, 96, 768), BF16)],
        [((896, 512), BF16)],
        2 * 8 * 896 * 128 * 512,
    )(rank, got, other_rims, filters)

    out = pl.pallas_call(
        sum_kernel,
        out_shape=jax.ShapeDtypeStruct((8, 128, 128), BF16),
        compiler_params=PARAMS,
        name="sum",
    )(keep, other)
    both = jnp.concatenate([grad, out], axis=1)
    both, planes, shifted = lax.optimization_barrier((both, planes, shifted))

    (terms,) = call(
        filter_grad_kernel,
        "filter_grad",
        [SCALAR, whole(10, 128, 512), whole(10, 96, 768)],
        [((4, 256, 128), BF16)],
        [((896, 512), BF16), ((128, 896), F32)],
        2 * 8 * 896 * 128 * 512,
    )(rank, planes, shifted)

    got = lax.all_to_all(both, "space", 0, 0, tiled=True)

    terms = (terms[:2].astype(F32) + swapped(terms[2:], "filt", 2).astype(F32)).astype(BF16)
    terms = (terms[0].astype(F32) + swapped(terms[1], "filt", 4).astype(F32)).astype(BF16)

    grad = jnp.sum(got[:, :512].astype(F32), axis=0).astype(BF16).reshape(64, 8, 128)
    out = with_corners(got[:, 512:].reshape(64, 2, 8, 128), terms.reshape(64, 2, 2, 128)).reshape(64, 16, 128)
    got = lax.all_to_all(jnp.concatenate([grad, out], axis=1), "filt", 0, 0, tiled=True)

    got = got.reshape(32, 2, 24, 128)
    grad = got[:, :, :8].reshape(32, 2, 2, 4, 128).transpose(1, 2, 0, 3, 4).reshape(4, 1, 128, 128)
    rims = got[:, :, 8:24].reshape(32, 2, 2, 8, 128)
    terms = jnp.sum(corners(rims).reshape(8, 4, 2, 4, 128).astype(F32), axis=0)
    terms = terms.reshape(2, 2, 2, 4, 128).transpose(2, 0, 1, 3, 4).reshape(1, 4, 8, 128)
    terms = lax.all_to_all(jnp.broadcast_to(terms, (8, 4, 8, 128)), "space", 0, 0, tiled=True)
    filter_grad = pl.pallas_call(
        finish_kernel,
        out_shape=jax.ShapeDtypeStruct((4, 27, 256), F32),
        scratch_shapes=[pltpu.VMEM((8, 32, 128), F32)],
        compiler_params=PARAMS,
        name="finish",
    )(terms)

    out = overlapped(rims.transpose(1, 2, 0, 3, 4).astype(F32)).astype(BF16).reshape(4, 1, 128, 128)
    return (out, grad, filter_grad)


def solution(mesh):
    placed = (
        P("filt", "space", None, None),
        P("filt", "space"),
        P("filt", None, None),
        P("filt", "space", None, None),
    )
    return jax.shard_map(
        local,
        mesh=mesh,
        in_specs=placed,
        out_specs=(
            P("filt", "space", None, None),
            P("filt", "space", None, None),
            P("filt", None, None),
        ),
        check_vma=False,
    )
```

```python
import math

import jax
import jax.numpy as jnp
from jax import lax
from jax.experimental import pallas as pl
from jax.experimental.pallas import tpu as pltpu
from jax.sharding import PartitionSpec as P


F32 = jnp.float32
BF16 = jnp.bfloat16
PARAMS = pltpu.CompilerParams(vmem_limit_bytes=16 * 1024 * 1024)
UNROLL = 4


def select_rows(rows, source, columns):
    row = lax.broadcasted_iota(jnp.int32, (rows, 128), 0)[:, :1]
    col = lax.broadcasted_iota(jnp.int32, (rows, columns), 1)
    return jnp.where(source(row) == col, 1.0, 0.0).astype(BF16)


def moved(matrix, cells):
    return jnp.dot(matrix, cells, preferred_element_type=F32).astype(BF16)


def by_24(n):
    part = (n * 2731) >> 16
    return part, n - part * 24


def by_32(n):
    return n >> 5, (n >> 1) & 15, n & 1


def pack_first(n):
    part, m = by_24(n)
    r, core = part >> 1, part & 1
    i, w = (m - 8) >> 3, m & 7
    rim = 64 + i * 64 + r * 4 + w + 14
    corner = 192 + (r & 3) * 4 + i * 2 + (w >> 2)
    inner = (w >= 1) & (w <= 6)
    return core * 208 + jnp.where(m < 8, (m >> 2) * 32 + r * 4 + (m & 3), jnp.where(inner, rim, corner))


def message_row(n):
    cell = (n & 15) * 24 + (n >> 6) * 4 + ((n >> 4) & 3)
    w, g, i = by_32(n - 128)
    rim = g * 24 + i * 8 + w + 9
    g, corner = (n - 320) >> 2, (n - 320) & 3
    return jnp.where(n < 128, cell, jnp.where(n < 320, rim, g * 24 + 8 + (corner >> 1) * 8 + (corner & 1) * 7))


def matrix_row(n):
    g, m = by_24(n)
    i, w = (m - 8) >> 3, m & 7
    cell = (m >> 2) * 64 + (m & 3) * 16 + g
    rim = 128 + (w - 1) * 32 + g * 2 + i
    inner = (w >= 1) & (w <= 6)
    return jnp.where(m < 8, cell, jnp.where(inner, rim, 320 + g * 4 + i * 2 + (w >> 2)))


def slot(rank, quarter):
    x = ((rank >> 1) & 3) ^ quarter
    return ((x & 1) << 1) | (x >> 1)


def first_kernel(scales_ref, cells_ref, rims_ref, own_ref, out_ref, raw, cells, rims, sems):
    copies = [
        pltpu.make_async_copy(cells_ref, raw, sems.at[0]),
        pltpu.make_async_copy(rims_ref, rims.at[:, 16:144], sems.at[1]),
    ]
    for copy in copies:
        copy.start()
    order = select_rows(384, pack_first, 416)
    for n in range(4):
        rims[n, :16] = jnp.zeros((16, 128), BF16)
        rims[n, 144:] = jnp.zeros((16, 128), BF16)
    for copy in copies:
        copy.wait()
    for n in range(4):
        cells[n] = (raw[n].astype(F32) * scales_ref[0, n]).astype(BF16)
    for block in range(4):
        at = block * 32
        parts = []
        for core in range(2):
            parts += [cells[2 * core + i, at : at + 32] for i in range(2)]
            parts += [rims[2 * core + i, at : at + 64] for i in range(2)]
            parts.append(own_ref[core])
        out_ref[block * 384 : block * 384 + 384] = moved(order, jnp.concatenate(parts, axis=0))


def middle_kernel(got_ref, out_ref, corners_ref):
    order = select_rows(384, message_row, 384)
    for block in range(4):
        rows = moved(order, got_ref[block * 384 : block * 384 + 384])
        for i in range(2):
            for y in range(4):
                piece = rows[i * 64 + y * 16 : i * 64 + y * 16 + 16]
                for place in range(4):
                    out_ref[2 * place + i, y * 64 + block * 16 : y * 64 + block * 16 + 16] = piece
            out_ref[2 * block + i, 256:448] = rows[128:320]
        corners_ref[block * 64 : block * 64 + 64] = rows[320:384]


def filter_kernel(rank_ref, slots_ref, filter_ref, stacked_ref):
    rank = rank_ref[0]
    by_n = select_rows(256, lambda n: (n & 63) * 4 + (n >> 6), 256)
    for h in range(2):
        for part in range(2):
            lanes = moved(by_n, slots_ref[slot(rank, 2 * ((rank & 1) ^ part) + h)])
            for n in range(4 - h):
                at = (4 * h + n) * 128
                filter_ref[part * 64 : part * 64 + 64, at : at + 128] = lanes[n * 64 : n * 64 + 64]
    same = select_rows(128, lambda n: n, 128)
    turned = [
        lax.dot_general(
            same,
            filter_ref[:, j * 128 : j * 128 + 128],
            (((1,), (1,)), ((), ())),
            preferred_element_type=F32,
        ).astype(BF16)
        for j in range(7)
    ]
    turned = jnp.concatenate(turned, axis=0)
    for a in range(3):
        stacked_ref[:, a * 128 : a * 128 + 128] = turned[a * 288 : a * 288 + 288]


def plane_of(mine_ref, theirs_ref, z):
    halves = [
        jnp.concatenate([ref[z, y * 64 : y * 64 + 64] for y in range(4)], axis=1) for ref in (mine_ref, theirs_ref)
    ]
    return jnp.concatenate(halves, axis=0)


def forward_kernel(mine_ref, theirs_ref, stacked_ref, out_ref, planes):
    planes[0] = jnp.zeros((128, 512), BF16)
    planes[9] = jnp.zeros((128, 512), BF16)
    for z in range(8):
        planes[z + 1] = plane_of(mine_ref, theirs_ref, z)
    column = lax.broadcasted_iota(jnp.int32, (32, 128), 1)

    def plane(z, _):
        near = jnp.concatenate([planes[z], planes[z + 1], planes[z + 2]], axis=0)
        terms = jnp.dot(stacked_ref[...], near, preferred_element_type=F32)
        for row in range(6):
            sums = []
            for e in range(3):
                total = None
                for b in range(3):
                    y = row + b - 2
                    if 0 <= y < 4:
                        at = b * 96 + e * 32
                        term = terms[at : at + 32, y * 128 : y * 128 + 128]
                        total = term if total is None else total + term
                sums.append(total)
            left = jnp.where(column >= 1, pltpu.roll(sums[0], 1, 1), 0.0)
            right = jnp.where(column <= 126, pltpu.roll(sums[2], 127, 1), 0.0)
            out_ref[z, 256 + row * 32 : 256 + row * 32 + 32] = (sums[1] + left + right).astype(BF16)
        return 0

    lax.fori_loop(0, 8, plane, 0, unroll=UNROLL)


def fill_image(image, shifted, z):
    for a in range(3):
        for b in range(3):
            at = (a * 3 + b) * 96
            image[at : at + 96] = shifted[z + 2 - a, :, (2 - b) * 128 : (2 - b) * 128 + 512]


def shift(got_ref, shifted):
    before = select_rows(128, lambda n: n - 1, 128)
    after = select_rows(128, lambda n: n + 1, 128)
    shifted[0] = jnp.zeros((96, 768), BF16)
    shifted[9] = jnp.zeros((96, 768), BF16)

    def plane(z, _):
        rows = got_ref[z, 256:448]
        for e, cells in ((0, moved(rows, before)), (1, rows), (2, moved(rows, after))):
            for y in range(6):
                shifted[z + 1, e * 32 : e * 32 + 32, y * 128 : y * 128 + 128] = cells[y * 32 : y * 32 + 32]
        return 0

    lax.fori_loop(0, 8, plane, 0, unroll=UNROLL)


def backward_kernel(got_ref, filter_ref, keep_ref, send_ref, shifted, image):
    shift(got_ref, shifted)
    image[864:896] = jnp.zeros((32, 512), BF16)

    def plane(z, _):
        fill_image(image, shifted, z)
        grad = jnp.dot(filter_ref[...], image[...], preferred_element_type=F32)
        for y in range(4):
            keep_ref[z, y * 64 : y * 64 + 64] = grad[:64, y * 128 : y * 128 + 128]
            send_ref[z, y * 64 : y * 64 + 64] = grad[64:, y * 128 : y * 128 + 128].astype(BF16)
        return 0

    lax.fori_loop(0, 8, plane, 0, unroll=UNROLL)


def sum_kernel(keep_ref, other_ref, out_ref, result_ref, rows_ref, sem):
    rows_ref[...] = (keep_ref[...] + other_ref[...].astype(F32)).astype(BF16)
    copy = pltpu.make_async_copy(rows_ref, result_ref.at[:, 0:256], sem)
    copy.start()
    copy.wait()


def filter_grad_kernel(rank_ref, got_ref, theirs_ref, slots_ref, shifted, image, total):
    shift(got_ref, shifted)
    image[864:896] = jnp.zeros((32, 512), BF16)
    total[...] = jnp.zeros((128, 896), F32)

    def plane(z, _):
        fill_image(image, shifted, z)
        total[...] += lax.dot_general(
            plane_of(got_ref, theirs_ref, z), image[...], (((1,), (1,)), ((), ())), preferred_element_type=F32
        )
        return 0

    lax.fori_loop(0, 8, plane, 0, unroll=UNROLL)
    back_n = select_rows(256, lambda n: (n & 3) * 64 + (n >> 2), 256)
    rank = rank_ref[0]
    for h in range(2):
        for part in range(2):
            rows = [
                total[part * 64 : part * 64 + 64, j * 128 : j * 128 + 128].astype(BF16)
                if j < 7
                else jnp.zeros((64, 128), BF16)
                for j in range(4 * h, 4 * h + 4)
            ]
            place = slot(rank, 2 * ((rank & 1) ^ part) + h)
            slots_ref[place] = moved(back_n, jnp.concatenate(rows, axis=0))


def last_kernel(got_ref, mine_ref, theirs_ref, out_ref, grads):
    order = select_rows(384, matrix_row, 384)
    for i in range(2):
        grad = got_ref[i, :256].astype(F32)
        for n in range(1, 4):
            grad = grad + got_ref[2 * n + i, :256].astype(F32)
        grads[i] = grad.astype(BF16)
    for block in range(4):
        parts = []
        for i in range(2):
            parts += [grads[i, y * 64 + block * 16 : y * 64 + block * 16 + 16] for y in range(4)]
        rims = [got_ref[2 * block + i, 256:448].astype(F32) for i in range(2)]
        parts.append((rims[0] + rims[1]).astype(BF16))
        part = slice(block * 64, block * 64 + 64)
        parts.append((mine_ref[part].astype(F32) + theirs_ref[part].astype(F32)).astype(BF16))
        out_ref[block * 384 : block * 384 + 384] = moved(order, jnp.concatenate(parts, axis=0))


def finish_kernel(parts_ref, out_ref, by_tap):
    row = lax.broadcasted_iota(jnp.int32, (256, 128), 0)
    lane = lax.broadcasted_iota(jnp.int32, (256, 128), 1)
    low = lax.broadcasted_iota(jnp.int32, (8, 128), 1) < 64
    norm = 1.0 / math.sqrt(131072)
    rows = []
    for c in range(2):
        for x in range(2):
            for y in range(4):
                rows.append(jnp.concatenate([parts_ref[2 * y + x, 2 * c + k] for k in range(2)], axis=1))
    rows = jnp.concatenate(rows, axis=0) * norm
    for pair in range(2):
        source = ((lane >> 1) & 1) * 128 + (2 * pair + (lane >> 6)) * 32 + ((lane >> 2) & 15) * 2 + (lane & 1)
        spread = jnp.where(source == row, 1.0, 0.0).astype(F32)
        wide = jnp.dot(rows, spread, preferred_element_type=F32, precision=lax.Precision.HIGHEST)
        for channel in range(4):
            for half in range(2):
                at = (channel * 4 + half * 2) * 8
                even, odd = wide[at : at + 8], wide[at + 8 : at + 16]
                by_tap[channel * 2 + half, pl.ds(2 * pair, 8, stride=4)] = jnp.where(low, even, pltpu.roll(odd, 64, 1))
                by_tap[channel * 2 + half, pl.ds(2 * pair + 1, 8, stride=4)] = jnp.where(
                    low, pltpu.roll(even, 64, 1), odd
                )
    for channel in range(4):
        for half in range(2):
            out_ref[:, channel, half * 128 : half * 128 + 128] = by_tap[channel * 2 + half, :27]


def overlapped(parts):
    lead = parts.shape[:-3]
    keep = [(0, 0)] * len(lead)
    first = jnp.pad(parts[..., 1:4, :], keep + [(0, 1), (1, 0), (0, 0)])
    second = jnp.pad(parts[..., 4:7, :], keep + [(1, 0), (0, 1), (0, 0)])
    return (first + second).reshape(lead + (132, 128))[..., 2:130, :]


def corners(rims):
    return jnp.concatenate([rims[..., :1, :], rims[..., 7:, :]], axis=-2)


def whole(*shape):
    return pl.BlockSpec(shape, lambda n: (0,) * len(shape))


SCALAR = pl.BlockSpec(memory_space=pltpu.SMEM)
ANY = pl.BlockSpec(memory_space=pl.ANY)
HBM = pl.BlockSpec(memory_space=pltpu.HBM)
DMA = pltpu.SemaphoreType.DMA


def call(kernel, name, ins, outs, scratch, flops, out_specs=None, aliases={}):
    return pl.pallas_call(
        kernel,
        grid=(1,),
        in_specs=ins,
        out_shape=[jax.ShapeDtypeStruct(shape, dtype) for shape, dtype in outs],
        out_specs=out_specs or [whole(*shape) for shape, _ in outs],
        scratch_shapes=[pltpu.VMEM(*s) if isinstance(s, tuple) else s for s in scratch],
        input_output_aliases=aliases,
        compiler_params=PARAMS,
        cost_estimate=pl.CostEstimate(flops=flops, bytes_accessed=4 << 20, transcendentals=0),
        name=name,
    )


def swapped(array, axis, bit):
    count = lax.axis_size(axis)
    return lax.ppermute(array, axis, [(n, n ^ bit) for n in range(count)])


def local(quantized, scales, weights, cotangent):
    rank = lax.axis_index("filt").reshape(1).astype(jnp.int32)
    slab = lax.axis_index("space")

    own = lax.dynamic_slice_in_dim(weights, slab // 2 * 64, 64, axis=2).reshape(2, 2, 27, 16, 2, 2)
    own = lax.dynamic_index_in_dim(own, slab % 2, axis=1, keepdims=False).transpose(3, 0, 1, 2, 4).reshape(2, 2, 864)
    own = jnp.pad(own, ((0, 0), (0, 0), (0, 160))).reshape(2, 16, 128)
    (both,) = call(
        first_kernel,
        "first",
        [SCALAR, HBM, HBM, whole(2, 16, 128)],
        [((1536, 128), BF16)],
        [((4, 128, 128), BF16), ((4, 128, 128), BF16), ((4, 160, 128), BF16), DMA((2,))],
        2 * 4 * 384 * 416 * 128,
    )(scales.reshape(1, 4), quantized.reshape(4, 128, 128), cotangent.reshape(4, 128, 128), own)
    got = lax.all_to_all(both.reshape(64, 24, 128), "filt", 0, 0, tiled=True)

    both, filters = call(
        middle_kernel,
        "middle",
        [whole(1536, 128)],
        [((8, 448, 128), BF16), ((256, 128), BF16)],
        [],
        2 * 4 * 384 * 384 * 128,
    )(got.reshape(1536, 128))
    got = lax.all_to_all(both, "space", 0, 0, tiled=True)
    filters = filters[None]
    for bit in (4, 2):
        filters = jnp.concatenate([filters, swapped(filters, "filt", bit)], axis=0)
    filters, got = lax.optimization_barrier((filters, got))
    filters, stacked = call(
        filter_kernel,
        "filters",
        [SCALAR, whole(4, 256, 128)],
        [((128, 896), BF16), ((288, 384), BF16)],
        [],
        2 * 4 * 256 * 256 * 128,
    )(rank, filters)

    theirs = swapped(got[:, :256], "filt", 1)
    keep, send = call(
        backward_kernel,
        "backward",
        [whole(8, 448, 128), whole(128, 896)],
        [((8, 256, 128), F32), ((8, 256, 128), BF16)],
        [((10, 96, 768), BF16), ((896, 512), BF16)],
        2 * 8 * 896 * 128 * 512,
    )(got, filters)
    send, theirs = lax.optimization_barrier((send, theirs))
    other = swapped(send, "filt", 1)
    cells = pl.BlockSpec((8, 256, 128), lambda n: (0, 0, 0))
    (out,) = call(
        forward_kernel,
        "forward",
        [cells, whole(8, 256, 128), whole(288, 384)],
        [((8, 448, 128), BF16)],
        [((10, 128, 512), BF16)],
        2 * 8 * 288 * 384 * 512,
    )(got, theirs, stacked)
    (both,) = call(
        sum_kernel,
        "sum",
        [whole(8, 256, 128), whole(8, 256, 128), ANY],
        [((8, 448, 128), BF16)],
        [((8, 256, 128), BF16), DMA],
        8 * 256 * 128,
        [ANY],
        {2: 0},
    )(keep, other, out)
    both, cells, theirs = lax.optimization_barrier((both, got, theirs))

    (terms,) = call(
        filter_grad_kernel,
        "filter_grad",
        [SCALAR, whole(8, 448, 128), whole(8, 256, 128)],
        [((4, 256, 128), BF16)],
        [((10, 96, 768), BF16), ((896, 512), BF16), ((128, 896), F32)],
        2 * 8 * 896 * 128 * 512,
    )(rank, cells, theirs)

    got = lax.all_to_all(both, "space", 0, 0, tiled=True)
    terms = (terms[:2].astype(F32) + swapped(terms[2:], "filt", 2).astype(F32)).astype(BF16)
    (both,) = call(
        last_kernel,
        "last",
        [whole(8, 448, 128), whole(256, 128), whole(256, 128)],
        [((1536, 128), BF16)],
        [((2, 256, 128), BF16)],
        2 * 4 * 384 * 384 * 128,
    )(got, terms[0], swapped(terms[1], "filt", 4))
    got = lax.all_to_all(both.reshape(64, 24, 128), "filt", 0, 0, tiled=True)

    got = got.reshape(32, 2, 24, 128)
    rims = got[:, :, 8:24].reshape(32, 2, 2, 8, 128)
    terms = jnp.sum(corners(rims).reshape(8, 2, 2, 2, 4, 128).astype(F32), axis=0)
    terms = terms.transpose(0, 2, 1, 3, 4).reshape(1, 4, 8, 128)
    terms, got = lax.optimization_barrier((jnp.broadcast_to(terms, (8, 4, 8, 128)), got))
    terms = lax.all_to_all(terms, "space", 0, 0, tiled=True)
    filter_grad = pl.pallas_call(
        finish_kernel,
        out_shape=jax.ShapeDtypeStruct((27, 4, 256), F32),
        scratch_shapes=[pltpu.VMEM((8, 32, 128), F32)],
        compiler_params=PARAMS,
        name="finish",
    )(terms).transpose(1, 0, 2)

    grad = got[:, :, :8].reshape(32, 2, 2, 4, 128).transpose(1, 2, 0, 3, 4).reshape(4, 1, 128, 128)
    rims = got[:, :, 8:24].reshape(32, 2, 2, 8, 128)
    out = overlapped(rims.transpose(1, 2, 0, 3, 4).astype(F32)).astype(BF16).reshape(4, 1, 128, 128)
    return (out, grad, filter_grad)


def solution(mesh):
    placed = (
        P("filt", "space", None, None),
        P("filt", "space"),
        P("filt", None, None),
        P("filt", "space", None, None),
    )
    return jax.shard_map(
        local,
        mesh=mesh,
        in_specs=placed,
        out_specs=(
            P("filt", "space", None, None),
            P("filt", "space", None, None),
            P("filt", None, None),
        ),
        check_vma=False,
    )
```

```python
import math

import jax
import jax.numpy as jnp
from jax import lax
from jax.experimental import pallas as pl
from jax.experimental.pallas import tpu as pltpu
from jax.sharding import PartitionSpec as P


F32 = jnp.float32
BF16 = jnp.bfloat16
PARAMS = pltpu.CompilerParams(vmem_limit_bytes=16 * 1024 * 1024)
UNROLL = 4


def select_rows(rows, source, columns):
    row = lax.broadcasted_iota(jnp.int32, (rows, 128), 0)[:, :1]
    col = lax.broadcasted_iota(jnp.int32, (rows, columns), 1)
    return jnp.where(source(row) == col, 1.0, 0.0).astype(BF16)


def moved(matrix, cells):
    return jnp.dot(matrix, cells, preferred_element_type=F32).astype(BF16)


def by_24(n):
    part = (n * 2731) >> 16
    return part, n - part * 24


def by_32(n):
    return n >> 5, (n >> 1) & 15, n & 1


def pack_first(n):
    part, m = by_24(n)
    r, core = part >> 1, part & 1
    i, w = (m - 8) >> 3, m & 7
    rim = 64 + i * 64 + r * 4 + w + 14
    corner = 192 + (r & 3) * 4 + i * 2 + (w >> 2)
    inner = (w >= 1) & (w <= 6)
    return core * 208 + jnp.where(m < 8, (m >> 2) * 32 + r * 4 + (m & 3), jnp.where(inner, rim, corner))


def message_row(n):
    cell = (n & 15) * 24 + (n >> 6) * 4 + ((n >> 4) & 3)
    w, g, i = by_32(n - 128)
    rim = g * 24 + i * 8 + w + 9
    g, corner = (n - 320) >> 2, (n - 320) & 3
    return jnp.where(n < 128, cell, jnp.where(n < 320, rim, g * 24 + 8 + (corner >> 1) * 8 + (corner & 1) * 7))


def matrix_row(n):
    g, m = by_24(n)
    i, w = (m - 8) >> 3, m & 7
    cell = (m >> 2) * 64 + (m & 3) * 16 + g
    rim = 128 + (w - 1) * 32 + g * 2 + i
    inner = (w >= 1) & (w <= 6)
    return jnp.where(m < 8, cell, jnp.where(inner, rim, 320 + g * 4 + i * 2 + (w >> 2)))


def quarter_of(rank):
    return (rank >> 1) & 3


def own_rows(slab, weights_ref):
    lane = lax.broadcasted_iota(jnp.int32, (16, 128), 1) >> 5
    weights = jnp.concatenate([weights_ref[tap] for tap in range(27)], axis=0)
    result = []
    for core in range(2):
        source = lambda n: (slab >> 1) * 64 + ((n >> 1) & 15) * 4 + core * 2 + (n & 1)
        row = lax.broadcasted_iota(jnp.int32, (256, 128), 0)
        col = lax.broadcasted_iota(jnp.int32, (256, 128), 1)
        pick = jnp.where(source(col) == row, 1.0, 0.0).astype(BF16)
        picked = moved(weights, pick)
        rows = jnp.zeros((16, 128), F32)
        for tap in range(4):
            order = select_rows(16, lambda n: (4 * (n & 7) + tap) * 4 + (n >> 3) * 2 + (slab & 1), 108)
            rows = jnp.where(lane == tap, jnp.dot(order, picked, preferred_element_type=F32), rows)
        result.append(rows.astype(BF16))
    return result


def first_kernel(slab_ref, scales_ref, cells_ref, rims_ref, weights_ref, out_ref, raw, cells, rims, sems):
    copies = [
        pltpu.make_async_copy(cells_ref, raw, sems.at[0]),
        pltpu.make_async_copy(rims_ref, rims.at[:, 16:144], sems.at[1]),
    ]
    for copy in copies:
        copy.start()
    order = select_rows(384, pack_first, 416)
    own = own_rows(slab_ref[0], weights_ref)
    for n in range(4):
        rims[n, :16] = jnp.zeros((16, 128), BF16)
        rims[n, 144:] = jnp.zeros((16, 128), BF16)
    for copy in copies:
        copy.wait()
    for n in range(4):
        cells[n] = (raw[n].astype(F32) * scales_ref[0, n]).astype(BF16)
    for block in range(4):
        at = block * 32
        parts = []
        for core in range(2):
            parts += [cells[2 * core + i, at : at + 32] for i in range(2)]
            parts += [rims[2 * core + i, at : at + 64] for i in range(2)]
            parts.append(own[core])
        out_ref[block * 384 : block * 384 + 384] = moved(order, jnp.concatenate(parts, axis=0))


def middle_kernel(got_ref, out_ref, corners_ref):
    order = select_rows(384, message_row, 384)
    for block in range(4):
        rows = moved(order, got_ref[block * 384 : block * 384 + 384])
        for i in range(2):
            for y in range(4):
                piece = rows[i * 64 + y * 16 : i * 64 + y * 16 + 16]
                for place in range(4):
                    out_ref[2 * place + i, y * 64 + block * 16 : y * 64 + block * 16 + 16] = piece
            out_ref[2 * block + i, 256:448] = rows[128:320]
        corners_ref[block * 64 : block * 64 + 64] = rows[320:384]


def filter_kernel(rank_ref, own_ref, first_ref, second_ref, third_ref, filter_ref, stacked_ref, quarters):
    rank = rank_ref[0]
    for n, ref in enumerate((own_ref, first_ref, second_ref, third_ref)):
        quarters[quarter_of(rank) ^ n] = ref[...]
    by_n = select_rows(256, lambda n: (n & 63) * 4 + (n >> 6), 256)
    for h in range(2):
        for part in range(2):
            lanes = moved(by_n, quarters[2 * ((rank & 1) ^ part) + h])
            for n in range(4 - h):
                at = (4 * h + n) * 128
                filter_ref[part * 64 : part * 64 + 64, at : at + 128] = lanes[n * 64 : n * 64 + 64]
    same = select_rows(128, lambda n: n, 128)
    turned = [
        lax.dot_general(
            same,
            filter_ref[:, j * 128 : j * 128 + 128],
            (((1,), (1,)), ((), ())),
            preferred_element_type=F32,
        ).astype(BF16)
        for j in range(7)
    ]
    turned = jnp.concatenate(turned, axis=0)
    for a in range(3):
        stacked_ref[:, a * 128 : a * 128 + 128] = turned[a * 288 : a * 288 + 288]


def plane_of(mine_ref, theirs_ref, z):
    halves = [
        jnp.concatenate([ref[z, y * 64 : y * 64 + 64] for y in range(4)], axis=1) for ref in (mine_ref, theirs_ref)
    ]
    return jnp.concatenate(halves, axis=0)


def forward_kernel(mine_ref, theirs_ref, stacked_ref, out_ref, planes, rows, sems):
    planes[0] = jnp.zeros((128, 512), BF16)
    planes[9] = jnp.zeros((128, 512), BF16)
    for z in range(8):
        planes[z + 1] = plane_of(mine_ref, theirs_ref, z)
    column = lax.broadcasted_iota(jnp.int32, (32, 128), 1)

    def plane(z, _):
        near = jnp.concatenate([planes[z], planes[z + 1], planes[z + 2]], axis=0)
        terms = jnp.dot(stacked_ref[...], near, preferred_element_type=F32)
        for row in range(6):
            sums = []
            for e in range(3):
                total = None
                for b in range(3):
                    y = row + b - 2
                    if 0 <= y < 4:
                        at = b * 96 + e * 32
                        term = terms[at : at + 32, y * 128 : y * 128 + 128]
                        total = term if total is None else total + term
                sums.append(total)
            left = jnp.where(column >= 1, pltpu.roll(sums[0], 1, 1), 0.0)
            right = jnp.where(column <= 126, pltpu.roll(sums[2], 127, 1), 0.0)
            rows[z, row * 32 : row * 32 + 32] = (sums[1] + left + right).astype(BF16)
        return 0

    copies = []
    for half in range(2):
        lax.fori_loop(half * 4, half * 4 + 4, plane, 0, unroll=UNROLL)
        part = slice(half * 4, half * 4 + 4)
        copies.append(pltpu.make_async_copy(rows.at[part], out_ref.at[part, 256:448], sems.at[half]))
        copies[-1].start()
    for copy in copies:
        copy.wait()


def fill_image(image, shifted, z):
    for a in range(3):
        for b in range(3):
            at = (a * 3 + b) * 96
            image[at : at + 96] = shifted[z + 2 - a, :, (2 - b) * 128 : (2 - b) * 128 + 512]


def shift(got_ref, shifted):
    before = select_rows(128, lambda n: n - 1, 128)
    after = select_rows(128, lambda n: n + 1, 128)
    shifted[0] = jnp.zeros((96, 768), BF16)
    shifted[9] = jnp.zeros((96, 768), BF16)

    def plane(z, _):
        rows = got_ref[z, 256:448]
        for e, cells in ((0, moved(rows, before)), (1, rows), (2, moved(rows, after))):
            for y in range(6):
                shifted[z + 1, e * 32 : e * 32 + 32, y * 128 : y * 128 + 128] = cells[y * 32 : y * 32 + 32]
        return 0

    lax.fori_loop(0, 8, plane, 0, unroll=UNROLL)


def backward_kernel(got_ref, filter_ref, keep_ref, send_ref, shifted, image):
    shift(got_ref, shifted)
    image[864:896] = jnp.zeros((32, 512), BF16)

    def plane(z, _):
        fill_image(image, shifted, z)
        grad = jnp.dot(filter_ref[...], image[...], preferred_element_type=F32)
        for y in range(4):
            keep_ref[z, y * 64 : y * 64 + 64] = grad[:64, y * 128 : y * 128 + 128]
            send_ref[z, y * 64 : y * 64 + 64] = grad[64:, y * 128 : y * 128 + 128].astype(BF16)
        return 0

    lax.fori_loop(0, 8, plane, 0, unroll=UNROLL)


def sum_kernel(keep_ref, other_ref, out_ref, result_ref, rows_ref, sems):
    copies = []
    for half in range(2):
        part = slice(half * 4, half * 4 + 4)
        rows_ref[part] = (keep_ref[part] + other_ref[part].astype(F32)).astype(BF16)
        copies.append(pltpu.make_async_copy(rows_ref.at[part], result_ref.at[part, 0:256], sems.at[half]))
        copies[-1].start()
    for copy in copies:
        copy.wait()


def filter_grad_kernel(
    rank_ref, got_ref, theirs_ref, own_ref, first_ref, second_ref, third_ref, shifted, image, total
):
    shift(got_ref, shifted)
    image[864:896] = jnp.zeros((32, 2048), BF16)
    total[...] = jnp.zeros((1024, 128), F32)
    for half in range(2):
        for z in range(4):
            fill_image(image.at[:, z * 512 : z * 512 + 512], shifted, half * 4 + z)
        cells = jnp.concatenate([plane_of(got_ref, theirs_ref, half * 4 + z) for z in range(4)], axis=1)
        total[:896] += lax.dot_general(image[...], cells, (((1,), (1,)), ((), ())), preferred_element_type=F32)
    rank = rank_ref[0]
    for n, ref in enumerate((own_ref, first_ref, second_ref, third_ref)):
        quarter = quarter_of(rank) ^ n
        part = ((quarter >> 1) ^ (rank & 1)) * 64
        order = select_rows(256, lambda n: (n & 3) * 128 + part + (n >> 2), 512)
        lanes = [
            total[pl.ds(pl.multiple_of((4 * (quarter & 1) + m) * 128, 128), 128)].astype(BF16) for m in range(4)
        ]
        ref[...] = lax.dot_general(
            order, jnp.concatenate(lanes, axis=1), (((1,), (1,)), ((), ())), preferred_element_type=F32
        ).astype(BF16)


def last_kernel(got_ref, own_ref, first_ref, second_ref, third_ref, out_ref, grads):
    order = select_rows(384, matrix_row, 384)
    for i in range(2):
        grad = got_ref[i, :256].astype(F32)
        for n in range(1, 4):
            grad = grad + got_ref[2 * n + i, :256].astype(F32)
        grads[i] = grad.astype(BF16)
    for block in range(4):
        parts = []
        for i in range(2):
            parts += [grads[i, y * 64 + block * 16 : y * 64 + block * 16 + 16] for y in range(4)]
        rims = [got_ref[2 * block + i, 256:448].astype(F32) for i in range(2)]
        parts.append((rims[0] + rims[1]).astype(BF16))
        part = slice(block * 64, block * 64 + 64)
        terms = [ref[part].astype(F32) for ref in (own_ref, first_ref, second_ref, third_ref)]
        parts.append(sum(terms[1:], terms[0]).astype(BF16))
        out_ref[block * 384 : block * 384 + 384] = moved(order, jnp.concatenate(parts, axis=0))


def tail_kernel(got_ref, out_ref):
    row = lax.broadcasted_iota(jnp.int32, (32, 1536), 0)
    col = lax.broadcasted_iota(jnp.int32, (32, 1536), 1)
    sender, m = by_24(col)
    corner = (m >= 8) & (((m & 7) == 0) | ((m & 7) == 7))
    n = ((m - 8) >> 3) * 2 + ((m & 7) >> 2)
    quarter = quarter_of(sender)
    target = (quarter >> 1) * 16 + (sender & 1) * 8 + (quarter & 1) * 4 + n
    order = jnp.where(corner & (target == row), 1.0, 0.0).astype(BF16)
    rows = jnp.dot(order, got_ref[...], preferred_element_type=F32)
    for n in range(8):
        out_ref[n] = rows


def finish_kernel(parts_ref, out_ref, by_tap):
    row = lax.broadcasted_iota(jnp.int32, (256, 128), 0)
    lane = lax.broadcasted_iota(jnp.int32, (256, 128), 1)
    low = lax.broadcasted_iota(jnp.int32, (8, 128), 1) < 64
    norm = 1.0 / math.sqrt(131072)
    rows = []
    for c in range(2):
        for x in range(2):
            for y in range(4):
                rows.append(jnp.concatenate([parts_ref[2 * y + x, 2 * c + k] for k in range(2)], axis=1))
    rows = jnp.concatenate(rows, axis=0) * norm
    for pair in range(2):
        source = ((lane >> 1) & 1) * 128 + (2 * pair + (lane >> 6)) * 32 + ((lane >> 2) & 15) * 2 + (lane & 1)
        spread = jnp.where(source == row, 1.0, 0.0).astype(F32)
        wide = jnp.dot(rows, spread, preferred_element_type=F32, precision=lax.Precision.HIGHEST)
        for channel in range(4):
            for half in range(2):
                at = (channel * 4 + half * 2) * 8
                even, odd = wide[at : at + 8], wide[at + 8 : at + 16]
                by_tap[channel * 2 + half, pl.ds(2 * pair, 8, stride=4)] = jnp.where(low, even, pltpu.roll(odd, 64, 1))
                by_tap[channel * 2 + half, pl.ds(2 * pair + 1, 8, stride=4)] = jnp.where(
                    low, pltpu.roll(even, 64, 1), odd
                )
    for channel in range(4):
        for half in range(2):
            out_ref[:, channel, half * 128 : half * 128 + 128] = by_tap[channel * 2 + half, :27]


def overlapped(parts):
    lead = parts.shape[:-3]
    keep = [(0, 0)] * len(lead)
    first = jnp.pad(parts[..., 1:4, :], keep + [(0, 1), (1, 0), (0, 0)])
    second = jnp.pad(parts[..., 4:7, :], keep + [(1, 0), (0, 1), (0, 0)])
    return (first + second).reshape(lead + (132, 128))[..., 2:130, :]


def whole(*shape):
    return pl.BlockSpec(shape, lambda n: (0,) * len(shape))


SCALAR = pl.BlockSpec(memory_space=pltpu.SMEM)
ANY = pl.BlockSpec(memory_space=pl.ANY)
HBM = pl.BlockSpec(memory_space=pltpu.HBM)
DMA = pltpu.SemaphoreType.DMA


def call(kernel, name, ins, outs, scratch, flops, out_specs=None, aliases={}, mib=16):
    return pl.pallas_call(
        kernel,
        grid=(1,),
        in_specs=ins,
        out_shape=[jax.ShapeDtypeStruct(shape, dtype) for shape, dtype in outs],
        out_specs=out_specs or [whole(*shape) for shape, _ in outs],
        scratch_shapes=[pltpu.VMEM(*s) if isinstance(s, tuple) else s for s in scratch],
        input_output_aliases=aliases,
        compiler_params=pltpu.CompilerParams(vmem_limit_bytes=mib * 1024 * 1024),
        cost_estimate=pl.CostEstimate(flops=flops, bytes_accessed=4 << 20, transcendentals=0),
        name=name,
    )


def swapped(array, axis, bit):
    count = lax.axis_size(axis)
    return lax.ppermute(array, axis, [(n, n ^ bit) for n in range(count)])


def local(quantized, scales, weights, cotangent):
    rank = lax.axis_index("filt").reshape(1).astype(jnp.int32)
    slab = lax.axis_index("space").reshape(1).astype(jnp.int32)

    (both,) = call(
        first_kernel,
        "first",
        [SCALAR, SCALAR, HBM, HBM, whole(27, 4, 256)],
        [((1536, 128), BF16)],
        [((4, 128, 128), BF16), ((4, 128, 128), BF16), ((4, 160, 128), BF16), DMA((2,))],
        2 * 4 * 384 * 416 * 128,
        mib=56,
    )(
        slab,
        scales.reshape(1, 4),
        quantized.reshape(4, 128, 128),
        cotangent.reshape(4, 128, 128),
        weights.transpose(1, 0, 2),
    )
    got = lax.all_to_all(both.reshape(64, 24, 128), "filt", 0, 0, tiled=True)

    both, filters = call(
        middle_kernel,
        "middle",
        [whole(1536, 128)],
        [((8, 448, 128), BF16), ((256, 128), BF16)],
        [],
        2 * 4 * 384 * 384 * 128,
    )(got.reshape(1536, 128))
    got = lax.all_to_all(both, "space", 0, 0, tiled=True)
    filters = [filters] + [swapped(filters, "filt", 2 * n) for n in range(1, 4)]
    filters, stacked = call(
        filter_kernel,
        "filters",
        [SCALAR] + [whole(256, 128)] * 4,
        [((128, 896), BF16), ((288, 384), BF16)],
        [((4, 256, 128), BF16)],
        2 * 4 * 256 * 256 * 128,
    )(rank, *filters)

    filters, stacked, got = lax.optimization_barrier((filters, stacked, got))
    theirs = swapped(got[:, :256], "filt", 1)
    keep, send = call(
        backward_kernel,
        "backward",
        [whole(8, 448, 128), whole(128, 896)],
        [((8, 256, 128), F32), ((8, 256, 128), BF16)],
        [((10, 96, 768), BF16), ((896, 512), BF16)],
        2 * 8 * 896 * 128 * 512,
    )(got, filters)
    send, theirs = lax.optimization_barrier((send, theirs))
    other = swapped(send, "filt", 1)
    cells = pl.BlockSpec((8, 256, 128), lambda n: (0, 0, 0))
    (out,) = call(
        forward_kernel,
        "forward",
        [cells, whole(8, 256, 128), whole(288, 384)],
        [((8, 448, 128), BF16)],
        [((10, 128, 512), BF16), ((8, 192, 128), BF16), DMA((2,))],
        2 * 8 * 288 * 384 * 512,
        [ANY],
    )(got, theirs, stacked)
    (both,) = call(
        sum_kernel,
        "sum",
        [whole(8, 256, 128), whole(8, 256, 128), ANY],
        [((8, 448, 128), BF16)],
        [((8, 256, 128), BF16), DMA((2,))],
        8 * 256 * 128,
        [ANY],
        {2: 0},
    )(keep, other, out)
    both, cells, theirs = lax.optimization_barrier((both, got, theirs))

    terms = call(
        filter_grad_kernel,
        "filter_grad",
        [SCALAR, whole(8, 448, 128), whole(8, 256, 128)],
        [((256, 128), BF16)] * 4,
        [((10, 96, 768), BF16), ((896, 2048), BF16), ((1024, 128), F32)],
        2 * 8 * 896 * 128 * 512,
    )(rank, cells, theirs)

    got = lax.all_to_all(both, "space", 0, 0, tiled=True)
    terms = [terms[0]] + [swapped(terms[n], "filt", 2 * n) for n in range(1, 4)]
    (both,) = call(
        last_kernel,
        "last",
        [whole(8, 448, 128)] + [whole(256, 128)] * 4,
        [((1536, 128), BF16)],
        [((2, 256, 128), BF16)],
        2 * 4 * 384 * 384 * 128,
    )(got, *terms)
    got = lax.all_to_all(both.reshape(64, 24, 128), "filt", 0, 0, tiled=True)

    (terms,) = call(
        tail_kernel, "tail", [whole(1536, 128)], [((8, 32, 128), F32)], [], 2 * 32 * 1536 * 128
    )(got.reshape(1536, 128))
    terms, got = lax.optimization_barrier((terms, got.reshape(32, 2, 24, 128)))
    terms = lax.all_to_all(terms, "space", 0, 0, tiled=True).reshape(8, 4, 8, 128)
    filter_grad = pl.pallas_call(
        finish_kernel,
        out_shape=jax.ShapeDtypeStruct((27, 4, 256), F32),
        scratch_shapes=[pltpu.VMEM((8, 32, 128), F32)],
        compiler_params=PARAMS,
        name="finish",
    )(terms).transpose(1, 0, 2)

    grad = got[:, :, :8].reshape(32, 2, 2, 4, 128).transpose(1, 2, 0, 3, 4).reshape(4, 1, 128, 128)
    rims = got[:, :, 8:24].reshape(32, 2, 2, 8, 128)
    out = overlapped(rims.transpose(1, 2, 0, 3, 4).astype(F32)).astype(BF16).reshape(4, 1, 128, 128)
    return (out, grad, filter_grad)


def solution(mesh):
    placed = (
        P("filt", "space", None, None),
        P("filt", "space"),
        P("filt", None, None),
        P("filt", "space", None, None),
    )
    return jax.shard_map(
        local,
        mesh=mesh,
        in_specs=placed,
        out_specs=(
            P("filt", "space", None, None),
            P("filt", "space", None, None),
            P("filt", None, None),
        ),
        check_vma=False,
    )
```

```python
import math

import jax
import jax.numpy as jnp
from jax import lax
from jax.experimental import pallas as pl
from jax.experimental.pallas import tpu as pltpu
from jax.sharding import PartitionSpec as P


F32 = jnp.float32
BF16 = jnp.bfloat16
PARAMS = pltpu.CompilerParams(vmem_limit_bytes=16 * 1024 * 1024)
UNROLL = 4


def select_rows(rows, source, columns):
    row = lax.broadcasted_iota(jnp.int32, (rows, 128), 0)[:, :1]
    col = lax.broadcasted_iota(jnp.int32, (rows, columns), 1)
    return jnp.where(source(row) == col, 1.0, 0.0).astype(BF16)


def moved(matrix, cells):
    return jnp.dot(matrix, cells, preferred_element_type=F32).astype(BF16)


def by_24(n):
    part = (n * 2731) >> 16
    return part, n - part * 24


def by_32(n):
    return n >> 5, (n >> 1) & 15, n & 1


def pack_first(n):
    part, m = by_24(n)
    r, core = part >> 1, part & 1
    i, w = (m - 8) >> 3, m & 7
    rim = 64 + i * 64 + r * 4 + w + 14
    corner = 192 + (r & 3) * 4 + i * 2 + (w >> 2)
    inner = (w >= 1) & (w <= 6)
    return core * 208 + jnp.where(m < 8, (m >> 2) * 32 + r * 4 + (m & 3), jnp.where(inner, rim, corner))


def message_row(n):
    cell = (n & 15) * 24 + (n >> 6) * 4 + ((n >> 4) & 3)
    w, g, i = by_32(n - 128)
    rim = g * 24 + i * 8 + w + 9
    g, corner = (n - 320) >> 2, (n - 320) & 3
    return jnp.where(n < 128, cell, jnp.where(n < 320, rim, g * 24 + 8 + (corner >> 1) * 8 + (corner & 1) * 7))


def by_28(n):
    part = (n * 2341) >> 16
    return part, n - part * 28


def matrix_row(n):
    g, m = by_28(n)
    i, w = (m - 8) >> 3, m & 7
    cell = (m >> 2) * 64 + (m & 3) * 16 + g
    rim = 128 + (w - 1) * 32 + g * 2 + i
    rim = jnp.where((w >= 1) & (w <= 6), rim, 320 + g * 4 + i * 2 + (w >> 2))
    return jnp.where(m < 8, cell, jnp.where(m < 24, rim, 384 + g * 4 + m - 24))


def quarter_of(rank):
    return (rank >> 1) & 3


def own_rows(slab, weights_ref):
    lane = lax.broadcasted_iota(jnp.int32, (16, 128), 1) >> 5
    weights = jnp.concatenate([weights_ref[tap] for tap in range(27)], axis=0)
    result = []
    for core in range(2):
        source = lambda n: (slab >> 1) * 64 + ((n >> 1) & 15) * 4 + core * 2 + (n & 1)
        row = lax.broadcasted_iota(jnp.int32, (256, 128), 0)
        col = lax.broadcasted_iota(jnp.int32, (256, 128), 1)
        pick = jnp.where(source(col) == row, 1.0, 0.0).astype(BF16)
        picked = moved(weights, pick)
        rows = jnp.zeros((16, 128), F32)
        for tap in range(4):
            order = select_rows(16, lambda n: (4 * (n & 7) + tap) * 4 + (n >> 3) * 2 + (slab & 1), 108)
            rows = jnp.where(lane == tap, jnp.dot(order, picked, preferred_element_type=F32), rows)
        result.append(rows.astype(BF16))
    return result


def first_kernel(slab_ref, scales_ref, cells_ref, rims_ref, weights_ref, out_ref, raw, cells, rims, packed, sems):
    copies = [
        pltpu.make_async_copy(cells_ref, raw, sems.at[0]),
        pltpu.make_async_copy(rims_ref, rims.at[:, 16:144], sems.at[1]),
    ]
    for copy in copies:
        copy.start()
    order = select_rows(384, pack_first, 416)
    own = own_rows(slab_ref[0], weights_ref)
    for n in range(4):
        rims[n, :16] = jnp.zeros((16, 128), BF16)
        rims[n, 144:] = jnp.zeros((16, 128), BF16)
    for copy in copies:
        copy.wait()
    for n in range(4):
        cells[n] = (raw[n].astype(F32) * scales_ref[0, n]).astype(BF16)
    for block in range(4):
        at = block * 32
        parts = []
        for core in range(2):
            parts += [cells[2 * core + i, at : at + 32] for i in range(2)]
            parts += [rims[2 * core + i, at : at + 64] for i in range(2)]
            parts.append(own[core])
        part = slice(block * 384, block * 384 + 384)
        packed[part] = moved(order, jnp.concatenate(parts, axis=0))
        copies.append(pltpu.make_async_copy(packed.at[part], out_ref.at[part], sems.at[2 + block]))
        copies[-1].start()
    for copy in copies[2:]:
        copy.wait()


def middle_kernel(got_ref, out_ref, corners_ref, cells, rims, sems):
    order = select_rows(384, message_row, 384)
    copies = []
    for block in range(4):
        rows = moved(order, got_ref[block * 384 : block * 384 + 384])
        for i in range(2):
            for y in range(4):
                piece = rows[i * 64 + y * 16 : i * 64 + y * 16 + 16]
                cells[i, y * 64 + block * 16 : y * 64 + block * 16 + 16] = piece
        rims[block] = rows[128:320]
        for i in range(2):
            to = 2 * block + i
            copies.append(pltpu.make_async_copy(rims.at[block], out_ref.at[to, 256:448], sems.at[to]))
            copies[-1].start()
        corners_ref[block * 64 : block * 64 + 64] = rows[320:384]
    for to in range(8):
        copies.append(pltpu.make_async_copy(cells.at[to % 2], out_ref.at[to, 0:256], sems.at[8 + to]))
        copies[-1].start()
    for copy in copies:
        copy.wait()


def filter_kernel(rank_ref, own_ref, first_ref, second_ref, third_ref, filter_ref, stacked_ref, quarters):
    rank = rank_ref[0]
    for n, ref in enumerate((own_ref, first_ref, second_ref, third_ref)):
        quarters[quarter_of(rank) ^ n] = ref[...]
    by_n = select_rows(256, lambda n: (n & 63) * 4 + (n >> 6), 256)
    for h in range(2):
        for part in range(2):
            lanes = moved(by_n, quarters[2 * ((rank & 1) ^ part) + h])
            for n in range(4 - h):
                at = (4 * h + n) * 128
                filter_ref[part * 64 : part * 64 + 64, at : at + 128] = lanes[n * 64 : n * 64 + 64]
    same = select_rows(128, lambda n: n, 128)
    turned = [
        lax.dot_general(
            same,
            filter_ref[:, j * 128 : j * 128 + 128],
            (((1,), (1,)), ((), ())),
            preferred_element_type=F32,
        ).astype(BF16)
        for j in range(7)
    ]
    turned = jnp.concatenate(turned, axis=0)
    for a in range(3):
        stacked_ref[:, a * 128 : a * 128 + 128] = turned[a * 288 : a * 288 + 288]


def plane_of(mine_ref, theirs_ref, z):
    halves = [
        jnp.concatenate([ref[z, y * 64 : y * 64 + 64] for y in range(4)], axis=1) for ref in (mine_ref, theirs_ref)
    ]
    return jnp.concatenate(halves, axis=0)


def forward_kernel(mine_ref, theirs_ref, stacked_ref, out_ref, planes, rows, sems):
    planes[0] = jnp.zeros((128, 512), BF16)
    planes[9] = jnp.zeros((128, 512), BF16)
    for z in range(8):
        planes[z + 1] = plane_of(mine_ref, theirs_ref, z)
    column = lax.broadcasted_iota(jnp.int32, (32, 128), 1)

    def plane(z, _):
        near = jnp.concatenate([planes[z], planes[z + 1], planes[z + 2]], axis=0)
        terms = jnp.dot(stacked_ref[...], near, preferred_element_type=F32)
        for row in range(6):
            sums = []
            for e in range(3):
                total = None
                for b in range(3):
                    y = row + b - 2
                    if 0 <= y < 4:
                        at = b * 96 + e * 32
                        term = terms[at : at + 32, y * 128 : y * 128 + 128]
                        total = term if total is None else total + term
                sums.append(total)
            left = jnp.where(column >= 1, pltpu.roll(sums[0], 1, 1), 0.0)
            right = jnp.where(column <= 126, pltpu.roll(sums[2], 127, 1), 0.0)
            rows[z, row * 32 : row * 32 + 32] = (sums[1] + left + right).astype(BF16)
        return 0

    copies = []
    for half in range(2):
        lax.fori_loop(half * 4, half * 4 + 4, plane, 0, unroll=UNROLL)
        part = slice(half * 4, half * 4 + 4)
        copies.append(pltpu.make_async_copy(rows.at[part], out_ref.at[part, 256:448], sems.at[half]))
        copies[-1].start()
    for copy in copies:
        copy.wait()


def fill_image(image, shifted, z):
    for a in range(3):
        for b in range(3):
            at = (a * 3 + b) * 96
            image[at : at + 96] = shifted[z + 2 - a, :, (2 - b) * 128 : (2 - b) * 128 + 512]


def shift(got_ref, shifted):
    before = select_rows(128, lambda n: n - 1, 128)
    after = select_rows(128, lambda n: n + 1, 128)
    shifted[0] = jnp.zeros((96, 768), BF16)
    shifted[9] = jnp.zeros((96, 768), BF16)

    def plane(z, _):
        rows = got_ref[z, 256:448]
        for e, cells in ((0, moved(rows, before)), (1, rows), (2, moved(rows, after))):
            for y in range(6):
                shifted[z + 1, e * 32 : e * 32 + 32, y * 128 : y * 128 + 128] = cells[y * 32 : y * 32 + 32]
        return 0

    lax.fori_loop(0, 8, plane, 0, unroll=UNROLL)


def backward_kernel(got_ref, filter_ref, keep_ref, send_ref, shifted, image):
    shift(got_ref, shifted)
    image[864:896] = jnp.zeros((32, 512), BF16)

    def plane(z, _):
        fill_image(image, shifted, z)
        grad = jnp.dot(filter_ref[...], image[...], preferred_element_type=F32)
        for y in range(4):
            keep_ref[z, y * 64 : y * 64 + 64] = grad[:64, y * 128 : y * 128 + 128]
            send_ref[z, y * 64 : y * 64 + 64] = grad[64:, y * 128 : y * 128 + 128].astype(BF16)
        return 0

    lax.fori_loop(0, 8, plane, 0, unroll=UNROLL)


def sum_kernel(keep_ref, other_ref, out_ref, result_ref, rows_ref, sems):
    copies = []
    for half in range(2):
        part = slice(half * 4, half * 4 + 4)
        rows_ref[part] = (keep_ref[part] + other_ref[part].astype(F32)).astype(BF16)
        copies.append(pltpu.make_async_copy(rows_ref.at[part], result_ref.at[part, 0:256], sems.at[half]))
        copies[-1].start()
    for copy in copies:
        copy.wait()


def filter_grad_kernel(rank_ref, got_ref, theirs_ref, own_ref, send_ref, shifted, image, total):
    shift(got_ref, shifted)
    image[864:896] = jnp.zeros((32, 2048), BF16)
    total[...] = jnp.zeros((1024, 128), F32)
    for half in range(2):
        for z in range(4):
            fill_image(image.at[:, z * 512 : z * 512 + 512], shifted, half * 4 + z)
        cells = jnp.concatenate([plane_of(got_ref, theirs_ref, half * 4 + z) for z in range(4)], axis=1)
        total[:896] += lax.dot_general(image[...], cells, (((1,), (1,)), ((), ())), preferred_element_type=F32)
    rank = rank_ref[0]
    for n, ref in enumerate((own_ref, send_ref)):
        part = (((rank >> 1) ^ n ^ rank) & 1) * 64
        order = select_rows(256, lambda n: (n & 3) * 128 + part + (n >> 2), 512)
        for h in range(2):
            lanes = [total[j * 128 : j * 128 + 128].astype(BF16) for j in range(4 * h, 4 * h + 4)]
            ref[h * 256 : h * 256 + 256] = lax.dot_general(
                order, jnp.concatenate(lanes, axis=1), (((1,), (1,)), ((), ())), preferred_element_type=F32
            ).astype(BF16)


def last_kernel(got_ref, own_ref, other_ref, out_ref, grads):
    order = select_rows(448, matrix_row, 448)
    for i in range(2):
        grad = got_ref[i, :256].astype(F32)
        for n in range(1, 4):
            grad = grad + got_ref[2 * n + i, :256].astype(F32)
        grads[i] = grad.astype(BF16)
    for block in range(4):
        parts = []
        for i in range(2):
            parts += [grads[i, y * 64 + block * 16 : y * 64 + block * 16 + 16] for y in range(4)]
        rims = [got_ref[2 * block + i, 256:448].astype(F32) for i in range(2)]
        parts.append((rims[0] + rims[1]).astype(BF16))
        for h in range(2):
            part = slice(h * 256 + block * 64, h * 256 + block * 64 + 64)
            parts.append((own_ref[part].astype(F32) + other_ref[part].astype(F32)).astype(BF16))
        out_ref[block * 448 : block * 448 + 448] = moved(order, jnp.concatenate(parts, axis=0))


def tail_kernel(got_ref, out_ref):
    row = lax.broadcasted_iota(jnp.int32, (32, 1792), 0)
    col = lax.broadcasted_iota(jnp.int32, (32, 1792), 1)
    sender, m = by_28(col)
    corner = (m >= 8) & (((m & 7) == 0) | ((m & 7) == 7) | (m >= 24))
    n = jnp.where(m < 24, ((m - 8) >> 3) * 2 + ((m & 7) >> 2), m - 20)
    target = ((sender >> 1) & 1) * 16 + (sender & 1) * 8 + n
    order = jnp.where(corner & (target == row), 1.0, 0.0).astype(BF16)
    rows = jnp.dot(order, got_ref[...], preferred_element_type=F32)
    for n in range(8):
        out_ref[n] = rows


def finish_kernel(parts_ref, out_ref, by_tap):
    row = lax.broadcasted_iota(jnp.int32, (256, 128), 0)
    lane = lax.broadcasted_iota(jnp.int32, (256, 128), 1)
    low = lax.broadcasted_iota(jnp.int32, (8, 128), 1) < 64
    norm = 1.0 / math.sqrt(131072)
    rows = []
    for c in range(2):
        for x in range(2):
            for y in range(4):
                rows.append(jnp.concatenate([parts_ref[2 * y + x, 2 * c + k] for k in range(2)], axis=1))
    rows = jnp.concatenate(rows, axis=0) * norm
    for pair in range(2):
        source = ((lane >> 1) & 1) * 128 + (2 * pair + (lane >> 6)) * 32 + ((lane >> 2) & 15) * 2 + (lane & 1)
        spread = jnp.where(source == row, 1.0, 0.0).astype(F32)
        wide = jnp.dot(rows, spread, preferred_element_type=F32, precision=lax.Precision.HIGHEST)
        for channel in range(4):
            for half in range(2):
                at = (channel * 4 + half * 2) * 8
                even, odd = wide[at : at + 8], wide[at + 8 : at + 16]
                by_tap[channel * 2 + half, pl.ds(2 * pair, 8, stride=4)] = jnp.where(low, even, pltpu.roll(odd, 64, 1))
                by_tap[channel * 2 + half, pl.ds(2 * pair + 1, 8, stride=4)] = jnp.where(
                    low, pltpu.roll(even, 64, 1), odd
                )
    for channel in range(4):
        for half in range(2):
            out_ref[:, channel, half * 128 : half * 128 + 128] = by_tap[channel * 2 + half, :27]


def overlapped(parts):
    lead = parts.shape[:-3]
    keep = [(0, 0)] * len(lead)
    first = jnp.pad(parts[..., 1:4, :], keep + [(0, 1), (1, 0), (0, 0)])
    second = jnp.pad(parts[..., 4:7, :], keep + [(1, 0), (0, 1), (0, 0)])
    return (first + second).reshape(lead + (132, 128))[..., 2:130, :]


def whole(*shape):
    return pl.BlockSpec(shape, lambda n: (0,) * len(shape))


SCALAR = pl.BlockSpec(memory_space=pltpu.SMEM)
ANY = pl.BlockSpec(memory_space=pl.ANY)
HBM = pl.BlockSpec(memory_space=pltpu.HBM)
DMA = pltpu.SemaphoreType.DMA


def call(kernel, name, ins, outs, scratch, flops, out_specs=None, aliases={}, mib=16):
    return pl.pallas_call(
        kernel,
        grid=(1,),
        in_specs=ins,
        out_shape=[jax.ShapeDtypeStruct(shape, dtype) for shape, dtype in outs],
        out_specs=out_specs or [whole(*shape) for shape, _ in outs],
        scratch_shapes=[pltpu.VMEM(*s) if isinstance(s, tuple) else s for s in scratch],
        input_output_aliases=aliases,
        compiler_params=pltpu.CompilerParams(vmem_limit_bytes=mib * 1024 * 1024),
        cost_estimate=pl.CostEstimate(flops=flops, bytes_accessed=4 << 20, transcendentals=0),
        name=name,
    )


def swapped(array, axis, bit):
    count = lax.axis_size(axis)
    return lax.ppermute(array, axis, [(n, n ^ bit) for n in range(count)])


def local(quantized, scales, weights, cotangent):
    rank = lax.axis_index("filt").reshape(1).astype(jnp.int32)
    slab = lax.axis_index("space").reshape(1).astype(jnp.int32)

    (both,) = call(
        first_kernel,
        "first",
        [SCALAR, SCALAR, HBM, HBM, whole(27, 4, 256)],
        [((1536, 128), BF16)],
        [((4, 128, 128), BF16), ((4, 128, 128), BF16), ((4, 160, 128), BF16), ((1536, 128), BF16), DMA((6,))],
        2 * 4 * 384 * 416 * 128,
        [HBM],
        mib=56,
    )(
        slab,
        scales.reshape(1, 4),
        quantized.reshape(4, 128, 128),
        cotangent.reshape(4, 128, 128),
        weights.transpose(1, 0, 2),
    )
    got = lax.all_to_all(both.reshape(64, 24, 128), "filt", 0, 0, tiled=True)

    both, filters = call(
        middle_kernel,
        "middle",
        [whole(1536, 128)],
        [((8, 448, 128), BF16), ((256, 128), BF16)],
        [((2, 256, 128), BF16), ((4, 192, 128), BF16), DMA((16,))],
        2 * 4 * 384 * 384 * 128,
        [HBM, whole(256, 128)],
    )(got.reshape(1536, 128))
    got = lax.all_to_all(both, "space", 0, 0, tiled=True)
    filters = [filters] + [swapped(filters, "filt", 2 * n) for n in range(1, 4)]
    filters, stacked = call(
        filter_kernel,
        "filters",
        [SCALAR] + [whole(256, 128)] * 4,
        [((128, 896), BF16), ((288, 384), BF16)],
        [((4, 256, 128), BF16)],
        2 * 4 * 256 * 256 * 128,
    )(rank, *filters)

    filters, stacked, got = lax.optimization_barrier((filters, stacked, got))
    theirs = swapped(got[:, :256], "filt", 1)
    keep, send = call(
        backward_kernel,
        "backward",
        [whole(8, 448, 128), whole(128, 896)],
        [((8, 256, 128), F32), ((8, 256, 128), BF16)],
        [((10, 96, 768), BF16), ((896, 512), BF16)],
        2 * 8 * 896 * 128 * 512,
    )(got, filters)
    send, theirs = lax.optimization_barrier((send, theirs))
    other = swapped(send, "filt", 1)
    cells = pl.BlockSpec((8, 256, 128), lambda n: (0, 0, 0))
    (out,) = call(
        forward_kernel,
        "forward",
        [cells, whole(8, 256, 128), whole(288, 384)],
        [((8, 448, 128), BF16)],
        [((10, 128, 512), BF16), ((8, 192, 128), BF16), DMA((2,))],
        2 * 8 * 288 * 384 * 512,
        [ANY],
    )(got, theirs, stacked)
    (both,) = call(
        sum_kernel,
        "sum",
        [whole(8, 256, 128), whole(8, 256, 128), ANY],
        [((8, 448, 128), BF16)],
        [((8, 256, 128), BF16), DMA((2,))],
        8 * 256 * 128,
        [ANY],
        {2: 0},
    )(keep, other, out)
    both, cells, theirs = lax.optimization_barrier((both, got, theirs))

    terms = call(
        filter_grad_kernel,
        "filter_grad",
        [SCALAR, whole(8, 448, 128), whole(8, 256, 128)],
        [((512, 128), BF16)] * 2,
        [((10, 96, 768), BF16), ((896, 2048), BF16), ((1024, 128), F32)],
        2 * 8 * 896 * 128 * 512,
    )(rank, cells, theirs)

    got = lax.all_to_all(both, "space", 0, 0, tiled=True)
    (both,) = call(
        last_kernel,
        "last",
        [whole(8, 448, 128)] + [whole(512, 128)] * 2,
        [((1792, 128), BF16)],
        [((2, 256, 128), BF16)],
        2 * 4 * 384 * 384 * 128,
    )(got, terms[0], swapped(terms[1], "filt", 2))
    got = lax.all_to_all(both.reshape(448, 4, 128), "filt", 0, 0, tiled=True)

    (terms,) = call(
        tail_kernel, "tail", [whole(1792, 128)], [((8, 32, 128), F32)], [], 2 * 32 * 1792 * 128
    )(got.reshape(1792, 128))
    terms, got = lax.optimization_barrier((terms, got.reshape(32, 2, 28, 128)))
    terms = lax.all_to_all(terms, "space", 0, 0, tiled=True).reshape(8, 4, 8, 128)
    filter_grad = pl.pallas_call(
        finish_kernel,
        out_shape=jax.ShapeDtypeStruct((27, 4, 256), F32),
        scratch_shapes=[pltpu.VMEM((8, 32, 128), F32)],
        compiler_params=PARAMS,
        name="finish",
    )(terms).transpose(1, 0, 2)

    grad = got[:, :, :8].reshape(32, 2, 2, 4, 128).transpose(1, 2, 0, 3, 4).reshape(4, 1, 128, 128)
    rims = got[:, :, 8:24].reshape(32, 2, 2, 8, 128)
    out = overlapped(rims.transpose(1, 2, 0, 3, 4).astype(F32)).astype(BF16).reshape(4, 1, 128, 128)
    return (out, grad, filter_grad)


def solution(mesh):
    placed = (
        P("filt", "space", None, None),
        P("filt", "space"),
        P("filt", None, None),
        P("filt", "space", None, None),
    )
    return jax.shard_map(
        local,
        mesh=mesh,
        in_specs=placed,
        out_specs=(
            P("filt", "space", None, None),
            P("filt", "space", None, None),
            P("filt", None, None),
        ),
        check_vma=False,
    )
```

```python
import math

import jax
import jax.numpy as jnp
from jax import lax
from jax.experimental import pallas as pl
from jax.experimental.pallas import tpu as pltpu
from jax.sharding import PartitionSpec as P


F32 = jnp.float32
BF16 = jnp.bfloat16
PARAMS = pltpu.CompilerParams(vmem_limit_bytes=16 * 1024 * 1024)


def select_rows(rows, source, columns):
    row = lax.broadcasted_iota(jnp.int32, (rows, 128), 0)[:, :1]
    col = lax.broadcasted_iota(jnp.int32, (rows, columns), 1)
    return jnp.where(source(row) == col, 1.0, 0.0).astype(BF16)


def moved(matrix, cells):
    return jnp.dot(matrix, cells, preferred_element_type=F32).astype(BF16)


def by_24(n):
    part = (n * 2731) >> 16
    return part, n - part * 24


def by_32(n):
    return n >> 5, (n >> 1) & 15, n & 1


def pack_first(n):
    part, m = by_24(n)
    r, core = part >> 1, part & 1
    i, w = (m - 8) >> 3, m & 7
    rim = 64 + i * 64 + r * 4 + w + 14
    corner = 192 + (r & 3) * 4 + i * 2 + (w >> 2)
    inner = (w >= 1) & (w <= 6)
    return core * 208 + jnp.where(m < 8, (m >> 2) * 32 + r * 4 + (m & 3), jnp.where(inner, rim, corner))


def message_row(n):
    cell = (n & 15) * 24 + (n >> 6) * 4 + ((n >> 4) & 3)
    w, g, i = by_32(n - 128)
    rim = g * 24 + i * 8 + w + 9
    g, corner = (n - 320) >> 2, (n - 320) & 3
    return jnp.where(n < 128, cell, jnp.where(n < 320, rim, g * 24 + 8 + (corner >> 1) * 8 + (corner & 1) * 7))


def by_28(n):
    part = (n * 2341) >> 16
    return part, n - part * 28


def matrix_row(n):
    g, m = by_28(n)
    i, w = (m - 8) >> 3, m & 7
    cell = (m >> 2) * 64 + (m & 3) * 16 + g
    rim = 128 + (w - 1) * 32 + g * 2 + i
    rim = jnp.where((w >= 1) & (w <= 6), rim, 320 + g * 4 + i * 2 + (w >> 2))
    return jnp.where(m < 8, cell, jnp.where(m < 24, rim, 384 + g * 4 + m - 24))


def quarter_of(rank):
    return (rank >> 1) & 3


def own_rows(slab, weights_ref):
    lane = lax.broadcasted_iota(jnp.int32, (16, 128), 1) >> 5
    weights = jnp.concatenate([weights_ref[tap] for tap in range(27)], axis=0)
    result = []
    for core in range(2):
        source = lambda n: (slab >> 1) * 64 + ((n >> 1) & 15) * 4 + core * 2 + (n & 1)
        row = lax.broadcasted_iota(jnp.int32, (256, 128), 0)
        col = lax.broadcasted_iota(jnp.int32, (256, 128), 1)
        pick = jnp.where(source(col) == row, 1.0, 0.0).astype(BF16)
        picked = moved(weights, pick)
        rows = jnp.zeros((16, 128), F32)
        for tap in range(4):
            order = select_rows(16, lambda n: (4 * (n & 7) + tap) * 4 + (n >> 3) * 2 + (slab & 1), 108)
            rows = jnp.where(lane == tap, jnp.dot(order, picked, preferred_element_type=F32), rows)
        result.append(rows.astype(BF16))
    return result


def first_kernel(
    scales_ref, cells_ref, rims_ref, weights_ref, out_ref, scales, raw, cells, rims, weights, packed, sems
):
    copies = [
        pltpu.make_async_copy(cells_ref, raw, sems.at[0]),
        pltpu.make_async_copy(rims_ref, rims.at[:, 16:144], sems.at[1]),
        pltpu.make_async_copy(scales_ref, scales, sems.at[2]),
        pltpu.make_async_copy(weights_ref, weights, sems.at[3]),
    ]
    for copy in copies:
        copy.start()
    order = select_rows(384, pack_first, 416)
    for n in range(4):
        rims[n, :16] = jnp.zeros((16, 128), BF16)
        rims[n, 144:] = jnp.zeros((16, 128), BF16)
    for copy in copies:
        copy.wait()
    for n in range(4):
        cells[n] = (raw[n].astype(F32) * scales[:, n : n + 1]).astype(BF16)
    own = own_rows(lax.axis_index("space"), weights)
    for block in range(4):
        at = block * 32
        parts = []
        for core in range(2):
            parts += [cells[2 * core + i, at : at + 32] for i in range(2)]
            parts += [rims[2 * core + i, at : at + 64] for i in range(2)]
            parts.append(own[core])
        part = slice(block * 384, block * 384 + 384)
        packed[part] = moved(order, jnp.concatenate(parts, axis=0))
        copies.append(pltpu.make_async_copy(packed.at[part], out_ref.at[part], sems.at[4 + block]))
        copies[-1].start()
    for copy in copies[4:]:
        copy.wait()


def middle_kernel(got_ref, out_ref, corners_ref, cells, rims, sems):
    order = select_rows(384, message_row, 384)
    copies = []
    for block in range(4):
        rows = moved(order, got_ref[block * 384 : block * 384 + 384])
        for i in range(2):
            for y in range(4):
                piece = rows[i * 64 + y * 16 : i * 64 + y * 16 + 16]
                cells[i, y * 64 + block * 16 : y * 64 + block * 16 + 16] = piece
        rims[block] = rows[128:320]
        for i in range(2):
            to = 2 * block + i
            copies.append(pltpu.make_async_copy(rims.at[block], out_ref.at[to, 256:448], sems.at[to]))
            copies[-1].start()
        corners_ref[block * 64 : block * 64 + 64] = rows[320:384]
    for to in range(8):
        copies.append(pltpu.make_async_copy(cells.at[to % 2], out_ref.at[to, 0:256], sems.at[8 + to]))
        copies[-1].start()
    for copy in copies:
        copy.wait()


def filter_kernel(rank_ref, own_ref, first_ref, second_ref, third_ref, filter_ref, stacked_ref, quarters):
    rank = rank_ref[0]
    for n, ref in enumerate((own_ref, first_ref, second_ref, third_ref)):
        quarters[quarter_of(rank) ^ n] = ref[...]
    by_n = select_rows(256, lambda n: (n & 63) * 4 + (n >> 6), 256)
    for h in range(2):
        for part in range(2):
            lanes = moved(by_n, quarters[2 * ((rank & 1) ^ part) + h])
            for n in range(4 - h):
                at = (4 * h + n) * 128
                filter_ref[part * 64 : part * 64 + 64, at : at + 128] = lanes[n * 64 : n * 64 + 64]
    same = select_rows(128, lambda n: n, 128)
    turned = [
        lax.dot_general(
            same,
            filter_ref[:, j * 128 : j * 128 + 128],
            (((1,), (1,)), ((), ())),
            preferred_element_type=F32,
        ).astype(BF16)
        for j in range(7)
    ]
    turned = jnp.concatenate(turned, axis=0)
    for a in range(3):
        stacked_ref[:, a * 128 : a * 128 + 128] = turned[a * 288 : a * 288 + 288]


def plane_of(mine_ref, theirs_ref, z):
    halves = [
        jnp.concatenate([ref[z, y * 64 : y * 64 + 64] for y in range(4)], axis=1) for ref in (mine_ref, theirs_ref)
    ]
    return jnp.concatenate(halves, axis=0)


def forward_kernel(mine_ref, theirs_ref, stacked_ref, out_ref, planes, rows, sems):
    planes[0] = jnp.zeros((128, 512), BF16)
    planes[9] = jnp.zeros((128, 512), BF16)
    for z in range(8):
        planes[z + 1] = plane_of(mine_ref, theirs_ref, z)
    column = lax.broadcasted_iota(jnp.int32, (32, 128), 1)

    def plane(z):
        near = jnp.concatenate([planes[z], planes[z + 1], planes[z + 2]], axis=0)
        terms = jnp.dot(stacked_ref[...], near, preferred_element_type=F32)
        for row in range(6):
            sums = []
            for e in range(3):
                total = None
                for b in range(3):
                    y = row + b - 2
                    if 0 <= y < 4:
                        at = b * 96 + e * 32
                        term = terms[at : at + 32, y * 128 : y * 128 + 128]
                        total = term if total is None else total + term
                sums.append(total)
            left = jnp.where(column >= 1, pltpu.roll(sums[0], 1, 1), 0.0)
            right = jnp.where(column <= 126, pltpu.roll(sums[2], 127, 1), 0.0)
            rows[z, row * 32 : row * 32 + 32] = (sums[1] + left + right).astype(BF16)

    copies = []
    for z in range(8):
        plane(z)
        copies.append(pltpu.make_async_copy(rows.at[z], out_ref.at[z, 256:448], sems.at[z]))
        copies[-1].start()
    for copy in copies:
        copy.wait()


def fill_image(image, shifted, z):
    for a in range(3):
        for b in range(3):
            at = (a * 3 + b) * 96
            image[at : at + 96] = shifted[z + 2 - a, :, (2 - b) * 128 : (2 - b) * 128 + 512]


def shift(got_ref, shifted):
    before = select_rows(128, lambda n: n - 1, 128)
    after = select_rows(128, lambda n: n + 1, 128)
    shifted[0] = jnp.zeros((96, 768), BF16)
    shifted[9] = jnp.zeros((96, 768), BF16)

    for z in range(8):
        rows = got_ref[z, 256:448]
        for e, cells in ((0, moved(rows, before)), (1, rows), (2, moved(rows, after))):
            for y in range(6):
                shifted[z + 1, e * 32 : e * 32 + 32, y * 128 : y * 128 + 128] = cells[y * 32 : y * 32 + 32]


def backward_kernel(got_ref, filter_ref, keep_ref, send_ref, shifted, images):
    shift(got_ref, shifted)
    images[:, 864:896] = jnp.zeros((2, 32, 512), BF16)
    for z in range(8):
        image = images.at[z % 2]
        fill_image(image, shifted, z)
        grad = jnp.dot(filter_ref[...], image[...], preferred_element_type=F32)
        for y in range(4):
            keep_ref[z, y * 64 : y * 64 + 64] = grad[:64, y * 128 : y * 128 + 128]
            send_ref[z, y * 64 : y * 64 + 64] = grad[64:, y * 128 : y * 128 + 128].astype(BF16)


def sum_kernel(keep_ref, other_ref, out_ref, result_ref, rows_ref, sems):
    copies = []
    for n in range(4):
        part = slice(n * 2, n * 2 + 2)
        rows_ref[part] = (keep_ref[part] + other_ref[part].astype(F32)).astype(BF16)
        copies.append(pltpu.make_async_copy(rows_ref.at[part], result_ref.at[part, 0:256], sems.at[n]))
        copies[-1].start()
    for copy in copies:
        copy.wait()


def filter_grad_kernel(rank_ref, got_ref, theirs_ref, own_ref, send_ref, shifted, image, total):
    shift(got_ref, shifted)
    image[864:896] = jnp.zeros((32, 2048), BF16)
    total[...] = jnp.zeros((1024, 128), F32)
    for half in range(2):
        for z in range(4):
            fill_image(image.at[:, z * 512 : z * 512 + 512], shifted, half * 4 + z)
        cells = jnp.concatenate([plane_of(got_ref, theirs_ref, half * 4 + z) for z in range(4)], axis=1)
        total[:896] += lax.dot_general(image[...], cells, (((1,), (1,)), ((), ())), preferred_element_type=F32)
    rank = rank_ref[0]
    for n, ref in enumerate((own_ref, send_ref)):
        part = (((rank >> 1) ^ n ^ rank) & 1) * 64
        order = select_rows(256, lambda n: (n & 3) * 128 + part + (n >> 2), 512)
        for h in range(2):
            lanes = [total[j * 128 : j * 128 + 128].astype(BF16) for j in range(4 * h, 4 * h + 4)]
            ref[h * 256 : h * 256 + 256] = lax.dot_general(
                order, jnp.concatenate(lanes, axis=1), (((1,), (1,)), ((), ())), preferred_element_type=F32
            ).astype(BF16)


def last_kernel(got_ref, own_ref, other_ref, out_ref, grads):
    order = select_rows(448, matrix_row, 448)
    for i in range(2):
        grad = got_ref[i, :256].astype(F32)
        for n in range(1, 4):
            grad = grad + got_ref[2 * n + i, :256].astype(F32)
        grads[i] = grad.astype(BF16)
    for block in range(4):
        parts = []
        for i in range(2):
            parts += [grads[i, y * 64 + block * 16 : y * 64 + block * 16 + 16] for y in range(4)]
        rims = [got_ref[2 * block + i, 256:448].astype(F32) for i in range(2)]
        parts.append((rims[0] + rims[1]).astype(BF16))
        for h in range(2):
            part = slice(h * 256 + block * 64, h * 256 + block * 64 + 64)
            parts.append((own_ref[part].astype(F32) + other_ref[part].astype(F32)).astype(BF16))
        out_ref[block * 448 : block * 448 + 448] = moved(order, jnp.concatenate(parts, axis=0))


def tail_kernel(got_ref, out_ref):
    row = lax.broadcasted_iota(jnp.int32, (32, 1792), 0)
    col = lax.broadcasted_iota(jnp.int32, (32, 1792), 1)
    sender, m = by_28(col)
    corner = (m >= 8) & (((m & 7) == 0) | ((m & 7) == 7) | (m >= 24))
    n = jnp.where(m < 24, ((m - 8) >> 3) * 2 + ((m & 7) >> 2), m - 20)
    target = ((sender >> 1) & 1) * 16 + (sender & 1) * 8 + n
    order = jnp.where(corner & (target == row), 1.0, 0.0).astype(BF16)
    rows = jnp.dot(order, got_ref[...], preferred_element_type=F32)
    for n in range(8):
        out_ref[n] = rows


def finish_kernel(parts_ref, out_ref, by_tap):
    low = lax.broadcasted_iota(jnp.int32, (8, 128), 1) < 64
    norm = 1.0 / math.sqrt(131072)
    rows = []
    for c in range(2):
        for x in range(2):
            for y in range(4):
                rows.append(jnp.concatenate([parts_ref[2 * y + x, 2 * c + k] for k in range(2)], axis=1))
    rows = jnp.concatenate(rows, axis=0) * norm
    high = rows.astype(BF16)
    rest = rows - high.astype(F32)
    middle = rest.astype(BF16)
    low_bits = (rest - middle.astype(F32)).astype(BF16)
    row = lax.broadcasted_iota(jnp.int32, (256, 256), 0)
    lane = lax.broadcasted_iota(jnp.int32, (256, 256), 1)
    source = ((lane >> 1) & 1) * 128 + (lane >> 6) * 32 + ((lane >> 2) & 15) * 2 + (lane & 1)
    spread = jnp.where(source == row, 1.0, 0.0).astype(BF16)
    terms = jnp.dot(jnp.concatenate([high, middle, low_bits], axis=0), spread, preferred_element_type=F32)
    both = terms[:128] + (terms[128:256] + terms[256:])
    for pair in range(2):
        wide = both[:, pair * 128 : pair * 128 + 128]
        for channel in range(4):
            for half in range(2):
                at = (channel * 4 + half * 2) * 8
                even, odd = wide[at : at + 8], wide[at + 8 : at + 16]
                by_tap[channel * 2 + half, pl.ds(2 * pair, 8, stride=4)] = jnp.where(low, even, pltpu.roll(odd, 64, 1))
                by_tap[channel * 2 + half, pl.ds(2 * pair + 1, 8, stride=4)] = jnp.where(
                    low, pltpu.roll(even, 64, 1), odd
                )
    for channel in range(4):
        for half in range(2):
            out_ref[:, channel, half * 128 : half * 128 + 128] = by_tap[channel * 2 + half, :27]


def overlapped(parts):
    lead = parts.shape[:-3]
    keep = [(0, 0)] * len(lead)
    first = jnp.pad(parts[..., 1:4, :], keep + [(0, 1), (1, 0), (0, 0)])
    second = jnp.pad(parts[..., 4:7, :], keep + [(1, 0), (0, 1), (0, 0)])
    return (first + second).reshape(lead + (132, 128))[..., 2:130, :]


def whole(*shape):
    return pl.BlockSpec(shape, lambda n: (0,) * len(shape))


SCALAR = pl.BlockSpec(memory_space=pltpu.SMEM)
ANY = pl.BlockSpec(memory_space=pl.ANY)
HBM = pl.BlockSpec(memory_space=pltpu.HBM)
DMA = pltpu.SemaphoreType.DMA


def call(kernel, name, ins, outs, scratch, flops, out_specs=None, aliases={}, mib=16):
    return pl.pallas_call(
        kernel,
        grid=(1,),
        in_specs=ins,
        out_shape=[jax.ShapeDtypeStruct(shape, dtype) for shape, dtype in outs],
        out_specs=out_specs or [whole(*shape) for shape, _ in outs],
        scratch_shapes=[pltpu.VMEM(*s) if isinstance(s, tuple) else s for s in scratch],
        input_output_aliases=aliases,
        compiler_params=pltpu.CompilerParams(vmem_limit_bytes=mib * 1024 * 1024),
        cost_estimate=pl.CostEstimate(flops=flops, bytes_accessed=4 << 20, transcendentals=0),
        name=name,
    )


def swapped(array, axis, bit):
    count = lax.axis_size(axis)
    return lax.ppermute(array, axis, [(n, n ^ bit) for n in range(count)])


def local(quantized, scales, weights, cotangent):
    rank = lax.axis_index("filt").reshape(1).astype(jnp.int32)

    (both,) = call(
        first_kernel,
        "first",
        [HBM] * 4,
        [((1536, 128), BF16)],
        [
            ((1, 4), F32),
            ((4, 128, 128), BF16),
            ((4, 128, 128), BF16),
            ((4, 160, 128), BF16),
            ((27, 4, 256), BF16),
            ((1536, 128), BF16),
            DMA((8,)),
        ],
        2 * 4 * 384 * 416 * 128,
        [HBM],
        mib=56,
    )(
        scales.reshape(1, 4),
        quantized.reshape(4, 128, 128),
        cotangent.reshape(4, 128, 128),
        weights.transpose(1, 0, 2),
    )
    got = lax.all_to_all(both.reshape(64, 24, 128), "filt", 0, 0, tiled=True)

    both, filters = call(
        middle_kernel,
        "middle",
        [whole(1536, 128)],
        [((8, 448, 128), BF16), ((256, 128), BF16)],
        [((2, 256, 128), BF16), ((4, 192, 128), BF16), DMA((16,))],
        2 * 4 * 384 * 384 * 128,
        [HBM, whole(256, 128)],
    )(got.reshape(1536, 128))
    got = lax.all_to_all(both, "space", 0, 0, tiled=True)
    filters = [filters] + [swapped(filters, "filt", 2 * n) for n in range(1, 4)]
    filters, stacked = call(
        filter_kernel,
        "filters",
        [SCALAR] + [whole(256, 128)] * 4,
        [((128, 896), BF16), ((288, 384), BF16)],
        [((4, 256, 128), BF16)],
        2 * 4 * 256 * 256 * 128,
    )(rank, *filters)

    filters, stacked, got = lax.optimization_barrier((filters, stacked, got))
    theirs = swapped(got[:, :256], "filt", 1)
    keep, send = call(
        backward_kernel,
        "backward",
        [whole(8, 448, 128), whole(128, 896)],
        [((8, 256, 128), F32), ((8, 256, 128), BF16)],
        [((10, 96, 768), BF16), ((2, 896, 512), BF16)],
        2 * 8 * 896 * 128 * 512,
    )(got, filters)
    send, theirs = lax.optimization_barrier((send, theirs))
    other = swapped(send, "filt", 1)
    cells = pl.BlockSpec((8, 256, 128), lambda n: (0, 0, 0))
    (out,) = call(
        forward_kernel,
        "forward",
        [cells, whole(8, 256, 128), whole(288, 384)],
        [((8, 448, 128), BF16)],
        [((10, 128, 512), BF16), ((8, 192, 128), BF16), DMA((8,))],
        2 * 8 * 288 * 384 * 512,
        [ANY],
    )(got, theirs, stacked)
    (both,) = call(
        sum_kernel,
        "sum",
        [whole(8, 256, 128), whole(8, 256, 128), ANY],
        [((8, 448, 128), BF16)],
        [((8, 256, 128), BF16), DMA((4,))],
        8 * 256 * 128,
        [ANY],
        {2: 0},
    )(keep, other, out)
    both, cells, theirs = lax.optimization_barrier((both, got, theirs))

    terms = call(
        filter_grad_kernel,
        "filter_grad",
        [SCALAR, whole(8, 448, 128), whole(8, 256, 128)],
        [((512, 128), BF16)] * 2,
        [((10, 96, 768), BF16), ((896, 2048), BF16), ((1024, 128), F32)],
        2 * 8 * 896 * 128 * 512,
    )(rank, cells, theirs)

    got = lax.all_to_all(both, "space", 0, 0, tiled=True)
    (both,) = call(
        last_kernel,
        "last",
        [whole(8, 448, 128)] + [whole(512, 128)] * 2,
        [((1792, 128), BF16)],
        [((2, 256, 128), BF16)],
        2 * 4 * 384 * 384 * 128,
    )(got, terms[0], swapped(terms[1], "filt", 2))
    got = lax.all_to_all(both.reshape(448, 4, 128), "filt", 0, 0, tiled=True)

    (terms,) = call(
        tail_kernel, "tail", [whole(1792, 128)], [((8, 32, 128), F32)], [], 2 * 32 * 1792 * 128
    )(got.reshape(1792, 128))
    terms, got = lax.optimization_barrier((terms, got.reshape(32, 2, 28, 128)))
    terms = lax.all_to_all(terms, "space", 0, 0, tiled=True).reshape(8, 4, 8, 128)
    filter_grad = pl.pallas_call(
        finish_kernel,
        out_shape=jax.ShapeDtypeStruct((27, 4, 256), F32),
        scratch_shapes=[pltpu.VMEM((8, 32, 128), F32)],
        compiler_params=PARAMS,
        name="finish",
    )(terms).transpose(1, 0, 2)

    grad = got[:, :, :8].reshape(32, 2, 2, 4, 128).transpose(1, 2, 0, 3, 4).reshape(4, 1, 128, 128)
    rims = got[:, :, 8:24].reshape(32, 2, 2, 8, 128)
    out = overlapped(rims.transpose(1, 2, 0, 3, 4).astype(F32)).astype(BF16).reshape(4, 1, 128, 128)
    return (out, grad, filter_grad)


def solution(mesh):
    placed = (
        P("filt", "space", None, None),
        P("filt", "space"),
        P("filt", None, None),
        P("filt", "space", None, None),
    )
    return jax.shard_map(
        local,
        mesh=mesh,
        in_specs=placed,
        out_specs=(
            P("filt", "space", None, None),
            P("filt", "space", None, None),
            P("filt", None, None),
        ),
        check_vma=False,
    )
```

```python
import math

import jax
import jax.numpy as jnp
from jax import lax
from jax.experimental import pallas as pl
from jax.experimental.pallas import tpu as pltpu
from jax.sharding import PartitionSpec as P


F32 = jnp.float32
BF16 = jnp.bfloat16
PARAMS = pltpu.CompilerParams(vmem_limit_bytes=16 * 1024 * 1024)


def select_rows(rows, source, columns):
    row = lax.broadcasted_iota(jnp.int32, (rows, 128), 0)[:, :1]
    col = lax.broadcasted_iota(jnp.int32, (rows, columns), 1)
    return jnp.where(source(row) == col, 1.0, 0.0).astype(BF16)


def moved(matrix, cells):
    return jnp.dot(matrix, cells, preferred_element_type=F32).astype(BF16)


def by_24(n):
    part = (n * 2731) >> 16
    return part, n - part * 24


def by_32(n):
    return n >> 5, (n >> 1) & 15, n & 1


def pack_first(n):
    part, m = by_24(n)
    r, core = part >> 1, part & 1
    i, w = (m - 8) >> 3, m & 7
    rim = 64 + i * 64 + r * 4 + w + 14
    corner = 192 + (r & 3) * 4 + i * 2 + (w >> 2)
    inner = (w >= 1) & (w <= 6)
    return core * 208 + jnp.where(m < 8, (m >> 2) * 32 + r * 4 + (m & 3), jnp.where(inner, rim, corner))


def message_row(n):
    cell = (n & 15) * 24 + (n >> 6) * 4 + ((n >> 4) & 3)
    w, g, i = by_32(n - 128)
    rim = g * 24 + i * 8 + w + 9
    g, corner = (n - 320) >> 2, (n - 320) & 3
    return jnp.where(n < 128, cell, jnp.where(n < 320, rim, g * 24 + 8 + (corner >> 1) * 8 + (corner & 1) * 7))


def by_28(n):
    part = (n * 2341) >> 16
    return part, n - part * 28


def matrix_row(n):
    g, m = by_28(n)
    i, w = (m - 8) >> 3, m & 7
    cell = (m >> 2) * 64 + (m & 3) * 16 + g
    rim = 128 + (w - 1) * 32 + g * 2 + i
    rim = jnp.where((w >= 1) & (w <= 6), rim, 320 + g * 4 + i * 2 + (w >> 2))
    return jnp.where(m < 8, cell, jnp.where(m < 24, rim, 384 + g * 4 + m - 24))


def quarter_of(rank):
    return (rank >> 1) & 3


def own_rows(slab, weights_ref):
    lane = lax.broadcasted_iota(jnp.int32, (16, 128), 1) >> 5
    weights = jnp.concatenate([weights_ref[tap] for tap in range(27)], axis=0)
    result = []
    for core in range(2):
        source = lambda n: (slab >> 1) * 64 + ((n >> 1) & 15) * 4 + core * 2 + (n & 1)
        row = lax.broadcasted_iota(jnp.int32, (256, 128), 0)
        col = lax.broadcasted_iota(jnp.int32, (256, 128), 1)
        pick = jnp.where(source(col) == row, 1.0, 0.0).astype(BF16)
        picked = moved(weights, pick)
        rows = jnp.zeros((16, 128), F32)
        for tap in range(4):
            order = select_rows(16, lambda n: (4 * (n & 7) + tap) * 4 + (n >> 3) * 2 + (slab & 1), 108)
            rows = jnp.where(lane == tap, jnp.dot(order, picked, preferred_element_type=F32), rows)
        result.append(rows.astype(BF16))
    return result


def first_kernel(
    scales_ref, cells_ref, rims_ref, weights_ref, out_ref, scales, raw, cells, rims, weights, packed, sems
):
    copies = [
        pltpu.make_async_copy(cells_ref, raw, sems.at[0]),
        pltpu.make_async_copy(rims_ref, rims.at[:, 16:144], sems.at[1]),
        pltpu.make_async_copy(scales_ref, scales, sems.at[2]),
        pltpu.make_async_copy(weights_ref, weights, sems.at[3]),
    ]
    for copy in copies:
        copy.start()
    order = select_rows(384, pack_first, 416)
    for n in range(4):
        rims[n, :16] = jnp.zeros((16, 128), BF16)
        rims[n, 144:] = jnp.zeros((16, 128), BF16)
    for copy in copies:
        copy.wait()
    for n in range(4):
        cells[n] = (raw[n].astype(F32) * scales[:, n : n + 1]).astype(BF16)
    own = own_rows(lax.axis_index("space"), weights)
    for block in range(4):
        at = block * 32
        parts = []
        for core in range(2):
            parts += [cells[2 * core + i, at : at + 32] for i in range(2)]
            parts += [rims[2 * core + i, at : at + 64] for i in range(2)]
            parts.append(own[core])
        part = slice(block * 384, block * 384 + 384)
        packed[part] = moved(order, jnp.concatenate(parts, axis=0))
        copies.append(pltpu.make_async_copy(packed.at[part], out_ref.at[part], sems.at[4 + block]))
        copies[-1].start()
    for copy in copies[4:]:
        copy.wait()


def middle_kernel(got_ref, out_ref, corners_ref, cells, rims, sems):
    copies = []
    order = select_rows(128, message_row, 384)
    for block in range(4):
        rows = moved(order, got_ref[block * 384 : block * 384 + 384])
        for i in range(2):
            for y in range(4):
                piece = rows[i * 64 + y * 16 : i * 64 + y * 16 + 16]
                cells[i, y * 64 + block * 16 : y * 64 + block * 16 + 16] = piece
    for to in range(8):
        copies.append(pltpu.make_async_copy(cells.at[to % 2], out_ref.at[to, 0:256], sems.at[8 + to]))
        copies[-1].start()
    order = select_rows(256, lambda n: message_row(n + 128), 384)
    for block in range(4):
        rows = moved(order, got_ref[block * 384 : block * 384 + 384])
        rims[block] = rows[:192]
        for i in range(2):
            to = 2 * block + i
            copies.append(pltpu.make_async_copy(rims.at[block], out_ref.at[to, 256:448], sems.at[to]))
            copies[-1].start()
        corners_ref[block * 64 : block * 64 + 64] = rows[192:]
    for copy in copies:
        copy.wait()


def filter_kernel(rank_ref, own_ref, first_ref, second_ref, third_ref, filter_ref, stacked_ref, quarters):
    rank = rank_ref[0]
    for n, ref in enumerate((own_ref, first_ref, second_ref, third_ref)):
        quarters[quarter_of(rank) ^ n] = ref[...]
    by_n = select_rows(256, lambda n: (n & 63) * 4 + (n >> 6), 256)
    for h in range(2):
        for part in range(2):
            lanes = moved(by_n, quarters[2 * ((rank & 1) ^ part) + h])
            for n in range(4 - h):
                at = (4 * h + n) * 128
                filter_ref[part * 64 : part * 64 + 64, at : at + 128] = lanes[n * 64 : n * 64 + 64]
    same = select_rows(128, lambda n: n, 128)
    turned = [
        lax.dot_general(
            same,
            filter_ref[:, j * 128 : j * 128 + 128],
            (((1,), (1,)), ((), ())),
            preferred_element_type=F32,
        ).astype(BF16)
        for j in range(7)
    ]
    turned = jnp.concatenate(turned, axis=0)
    for a in range(3):
        stacked_ref[:, a * 128 : a * 128 + 128] = turned[a * 288 : a * 288 + 288]


def plane_of(mine_ref, theirs_ref, z):
    halves = [
        jnp.concatenate([ref[z, y * 64 : y * 64 + 64] for y in range(4)], axis=1) for ref in (mine_ref, theirs_ref)
    ]
    return jnp.concatenate(halves, axis=0)


def forward_kernel(mine_ref, theirs_ref, stacked_ref, out_ref, planes):
    planes[0] = jnp.zeros((128, 512), BF16)
    planes[9] = jnp.zeros((128, 512), BF16)
    for z in range(8):
        planes[z + 1] = plane_of(mine_ref, theirs_ref, z)
    column = lax.broadcasted_iota(jnp.int32, (32, 128), 1)

    def plane(z):
        near = jnp.concatenate([planes[z], planes[z + 1], planes[z + 2]], axis=0)
        terms = jnp.dot(stacked_ref[...], near, preferred_element_type=F32)
        for row in range(6):
            sums = []
            for e in range(3):
                total = None
                for b in range(3):
                    y = row + b - 2
                    if 0 <= y < 4:
                        at = b * 96 + e * 32
                        term = terms[at : at + 32, y * 128 : y * 128 + 128]
                        total = term if total is None else total + term
                sums.append(total)
            left = jnp.where(column >= 1, pltpu.roll(sums[0], 1, 1), 0.0)
            right = jnp.where(column <= 126, pltpu.roll(sums[2], 127, 1), 0.0)
            out_ref[z, row * 32 : row * 32 + 32] = (sums[1] + left + right).astype(BF16)

    for z in range(8):
        plane(z)


def fill_image(image, shifted, z):
    for a in range(3):
        for b in range(3):
            at = (a * 3 + b) * 96
            image[at : at + 96] = shifted[z + 2 - a, :, (2 - b) * 128 : (2 - b) * 128 + 512]


def shift(got_ref, shifted):
    before = select_rows(128, lambda n: n - 1, 128)
    after = select_rows(128, lambda n: n + 1, 128)
    shifted[0] = jnp.zeros((96, 768), BF16)
    shifted[9] = jnp.zeros((96, 768), BF16)

    for z in range(8):
        rows = got_ref[z, 256:448]
        for e, cells in ((0, moved(rows, before)), (1, rows), (2, moved(rows, after))):
            for y in range(6):
                shifted[z + 1, e * 32 : e * 32 + 32, y * 128 : y * 128 + 128] = cells[y * 32 : y * 32 + 32]


def backward_kernel(got_ref, filter_ref, keep_ref, send_ref, shifted, images):
    shift(got_ref, shifted)
    images[:, 864:896] = jnp.zeros((2, 32, 512), BF16)
    for z in range(8):
        image = images.at[z % 2]
        fill_image(image, shifted, z)
        grad = jnp.dot(filter_ref[...], image[...], preferred_element_type=F32)
        for y in range(4):
            keep_ref[z, y * 64 : y * 64 + 64] = grad[:64, y * 128 : y * 128 + 128]
            send_ref[z, y * 64 : y * 64 + 64] = grad[64:, y * 128 : y * 128 + 128].astype(BF16)


def sum_kernel(keep_ref, other_ref, rims_ref, out_ref, rows_ref, sems):
    copies = [pltpu.make_async_copy(rims_ref, out_ref.at[:, 256:448], sems.at[4])]
    copies[0].start()
    for n in range(4):
        part = slice(n * 2, n * 2 + 2)
        rows_ref[part] = (keep_ref[part] + other_ref[part].astype(F32)).astype(BF16)
        copies.append(pltpu.make_async_copy(rows_ref.at[part], out_ref.at[part, 0:256], sems.at[n]))
        copies[-1].start()
    for copy in copies:
        copy.wait()


def filter_grad_kernel(rank_ref, got_ref, theirs_ref, own_ref, send_ref, shifted, image, total):
    shift(got_ref, shifted)
    image[864:896] = jnp.zeros((32, 2048), BF16)
    total[...] = jnp.zeros((1024, 128), F32)
    for half in range(2):
        for z in range(4):
            fill_image(image.at[:, z * 512 : z * 512 + 512], shifted, half * 4 + z)
        cells = jnp.concatenate([plane_of(got_ref, theirs_ref, half * 4 + z) for z in range(4)], axis=1)
        total[:896] += lax.dot_general(image[...], cells, (((1,), (1,)), ((), ())), preferred_element_type=F32)
    rank = rank_ref[0]
    for n, ref in enumerate((own_ref, send_ref)):
        part = (((rank >> 1) ^ n ^ rank) & 1) * 64
        order = select_rows(256, lambda n: (n & 3) * 128 + part + (n >> 2), 512)
        for h in range(2):
            lanes = [total[j * 128 : j * 128 + 128].astype(BF16) for j in range(4 * h, 4 * h + 4)]
            ref[h * 256 : h * 256 + 256] = lax.dot_general(
                order, jnp.concatenate(lanes, axis=1), (((1,), (1,)), ((), ())), preferred_element_type=F32
            ).astype(BF16)


def last_kernel(got_ref, own_ref, other_ref, out_ref, grads):
    order = select_rows(448, matrix_row, 448)
    for i in range(2):
        grad = got_ref[i, :256].astype(F32)
        for n in range(1, 4):
            grad = grad + got_ref[2 * n + i, :256].astype(F32)
        grads[i] = grad.astype(BF16)
    for block in range(4):
        parts = []
        for i in range(2):
            parts += [grads[i, y * 64 + block * 16 : y * 64 + block * 16 + 16] for y in range(4)]
        rims = [got_ref[2 * block + i, 256:448].astype(F32) for i in range(2)]
        parts.append((rims[0] + rims[1]).astype(BF16))
        for h in range(2):
            part = slice(h * 256 + block * 64, h * 256 + block * 64 + 64)
            parts.append((own_ref[part].astype(F32) + other_ref[part].astype(F32)).astype(BF16))
        out_ref[block * 448 : block * 448 + 448] = moved(order, jnp.concatenate(parts, axis=0))


def tail_kernel(got_ref, out_ref):
    row = lax.broadcasted_iota(jnp.int32, (32, 1792), 0)
    col = lax.broadcasted_iota(jnp.int32, (32, 1792), 1)
    sender, m = by_28(col)
    corner = (m >= 8) & (((m & 7) == 0) | ((m & 7) == 7) | (m >= 24))
    n = jnp.where(m < 24, ((m - 8) >> 3) * 2 + ((m & 7) >> 2), m - 20)
    target = ((sender >> 1) & 1) * 16 + (sender & 1) * 8 + n
    order = jnp.where(corner & (target == row), 1.0, 0.0).astype(BF16)
    rows = jnp.dot(order, got_ref[...], preferred_element_type=F32)
    for n in range(8):
        out_ref[n] = rows


def finish_kernel(parts_ref, out_ref, by_tap):
    low = lax.broadcasted_iota(jnp.int32, (8, 128), 1) < 64
    norm = 1.0 / math.sqrt(131072)
    rows = []
    for c in range(2):
        for x in range(2):
            for y in range(4):
                rows.append(jnp.concatenate([parts_ref[2 * y + x, 2 * c + k] for k in range(2)], axis=1))
    rows = jnp.concatenate(rows, axis=0) * norm
    high = rows.astype(BF16)
    rest = rows - high.astype(F32)
    middle = rest.astype(BF16)
    low_bits = (rest - middle.astype(F32)).astype(BF16)
    row = lax.broadcasted_iota(jnp.int32, (256, 256), 0)
    lane = lax.broadcasted_iota(jnp.int32, (256, 256), 1)
    source = ((lane >> 1) & 1) * 128 + (lane >> 6) * 32 + ((lane >> 2) & 15) * 2 + (lane & 1)
    spread = jnp.where(source == row, 1.0, 0.0).astype(BF16)
    terms = jnp.dot(jnp.concatenate([high, middle, low_bits], axis=0), spread, preferred_element_type=F32)
    both = terms[:128] + (terms[128:256] + terms[256:])
    for pair in range(2):
        wide = both[:, pair * 128 : pair * 128 + 128]
        for channel in range(4):
            for half in range(2):
                at = (channel * 4 + half * 2) * 8
                even, odd = wide[at : at + 8], wide[at + 8 : at + 16]
                by_tap[channel * 2 + half, pl.ds(2 * pair, 8, stride=4)] = jnp.where(low, even, pltpu.roll(odd, 64, 1))
                by_tap[channel * 2 + half, pl.ds(2 * pair + 1, 8, stride=4)] = jnp.where(
                    low, pltpu.roll(even, 64, 1), odd
                )
    for channel in range(4):
        for half in range(2):
            out_ref[:, channel, half * 128 : half * 128 + 128] = by_tap[channel * 2 + half, :27]


def overlapped(parts):
    lead = parts.shape[:-3]
    keep = [(0, 0)] * len(lead)
    first = jnp.pad(parts[..., 1:4, :], keep + [(0, 1), (1, 0), (0, 0)])
    second = jnp.pad(parts[..., 4:7, :], keep + [(1, 0), (0, 1), (0, 0)])
    return (first + second).reshape(lead + (132, 128))[..., 2:130, :]


def whole(*shape):
    return pl.BlockSpec(shape, lambda n: (0,) * len(shape))


SCALAR = pl.BlockSpec(memory_space=pltpu.SMEM)
HBM = pl.BlockSpec(memory_space=pltpu.HBM)
DMA = pltpu.SemaphoreType.DMA


def call(kernel, name, ins, outs, scratch, flops, out_specs=None, mib=16):
    return pl.pallas_call(
        kernel,
        grid=(1,),
        in_specs=ins,
        out_shape=[jax.ShapeDtypeStruct(shape, dtype) for shape, dtype in outs],
        out_specs=out_specs or [whole(*shape) for shape, _ in outs],
        scratch_shapes=[pltpu.VMEM(*s) if isinstance(s, tuple) else s for s in scratch],
        compiler_params=pltpu.CompilerParams(vmem_limit_bytes=mib * 1024 * 1024),
        cost_estimate=pl.CostEstimate(flops=flops, bytes_accessed=4 << 20, transcendentals=0),
        name=name,
    )


def swapped(array, axis, bit):
    count = lax.axis_size(axis)
    return lax.ppermute(array, axis, [(n, n ^ bit) for n in range(count)])


def local(quantized, scales, weights, cotangent):
    rank = lax.axis_index("filt").reshape(1).astype(jnp.int32)

    (both,) = call(
        first_kernel,
        "first",
        [HBM] * 4,
        [((1536, 128), BF16)],
        [
            ((1, 4), F32),
            ((4, 128, 128), BF16),
            ((4, 128, 128), BF16),
            ((4, 160, 128), BF16),
            ((27, 4, 256), BF16),
            ((1536, 128), BF16),
            DMA((8,)),
        ],
        2 * 4 * 384 * 416 * 128,
        [HBM],
        mib=56,
    )(
        scales.reshape(1, 4),
        quantized.reshape(4, 128, 128),
        cotangent.reshape(4, 128, 128),
        weights.transpose(1, 0, 2),
    )
    got = lax.all_to_all(both.reshape(64, 24, 128), "filt", 0, 0, tiled=True)

    both, filters = call(
        middle_kernel,
        "middle",
        [whole(1536, 128)],
        [((8, 448, 128), BF16), ((256, 128), BF16)],
        [((2, 256, 128), BF16), ((4, 192, 128), BF16), DMA((16,))],
        2 * 4 * 384 * 384 * 128,
        [HBM, whole(256, 128)],
    )(got.reshape(1536, 128))
    got = lax.all_to_all(both, "space", 0, 0, tiled=True)
    filters = [filters] + [swapped(filters, "filt", 2 * n) for n in range(1, 4)]
    filters, stacked = call(
        filter_kernel,
        "filters",
        [SCALAR] + [whole(256, 128)] * 4,
        [((128, 896), BF16), ((288, 384), BF16)],
        [((4, 256, 128), BF16)],
        2 * 4 * 256 * 256 * 128,
    )(rank, *filters)

    filters, stacked, got = lax.optimization_barrier((filters, stacked, got))
    theirs = swapped(got[:, :256], "filt", 1)
    keep, send = call(
        backward_kernel,
        "backward",
        [whole(8, 448, 128), whole(128, 896)],
        [((8, 256, 128), F32), ((8, 256, 128), BF16)],
        [((10, 96, 768), BF16), ((2, 896, 512), BF16)],
        2 * 8 * 896 * 128 * 512,
    )(got, filters)
    send, theirs = lax.optimization_barrier((send, theirs))
    other = swapped(send, "filt", 1)
    cells = pl.BlockSpec((8, 256, 128), lambda n: (0, 0, 0))
    (out,) = call(
        forward_kernel,
        "forward",
        [cells, whole(8, 256, 128), whole(288, 384)],
        [((8, 192, 128), BF16)],
        [((10, 128, 512), BF16)],
        2 * 8 * 288 * 384 * 512,
    )(got, theirs, stacked)
    (both,) = call(
        sum_kernel,
        "sum",
        [whole(8, 256, 128), whole(8, 256, 128), whole(8, 192, 128)],
        [((8, 448, 128), BF16)],
        [((8, 256, 128), BF16), DMA((5,))],
        8 * 256 * 128,
        [HBM],
    )(keep, other, out)
    both, cells, theirs = lax.optimization_barrier((both, got, theirs))

    terms = call(
        filter_grad_kernel,
        "filter_grad",
        [SCALAR, whole(8, 448, 128), whole(8, 256, 128)],
        [((512, 128), BF16)] * 2,
        [((10, 96, 768), BF16), ((896, 2048), BF16), ((1024, 128), F32)],
        2 * 8 * 896 * 128 * 512,
    )(rank, cells, theirs)

    got = lax.all_to_all(both, "space", 0, 0, tiled=True)
    (both,) = call(
        last_kernel,
        "last",
        [whole(8, 448, 128)] + [whole(512, 128)] * 2,
        [((1792, 128), BF16)],
        [((2, 256, 128), BF16)],
        2 * 4 * 384 * 384 * 128,
    )(got, terms[0], swapped(terms[1], "filt", 2))
    got = lax.all_to_all(both.reshape(448, 4, 128), "filt", 0, 0, tiled=True)

    (terms,) = call(
        tail_kernel, "tail", [whole(1792, 128)], [((8, 32, 128), F32)], [], 2 * 32 * 1792 * 128
    )(got.reshape(1792, 128))
    terms, got = lax.optimization_barrier((terms, got.reshape(32, 2, 28, 128)))
    terms = lax.all_to_all(terms, "space", 0, 0, tiled=True).reshape(8, 4, 8, 128)
    filter_grad = pl.pallas_call(
        finish_kernel,
        out_shape=jax.ShapeDtypeStruct((27, 4, 256), F32),
        scratch_shapes=[pltpu.VMEM((8, 32, 128), F32)],
        compiler_params=PARAMS,
        name="finish",
    )(terms).transpose(1, 0, 2)

    grad = got[:, :, :8].reshape(32, 2, 2, 4, 128).transpose(1, 2, 0, 3, 4).reshape(4, 1, 128, 128)
    rims = got[:, :, 8:24].reshape(32, 2, 2, 8, 128)
    out = overlapped(rims.transpose(1, 2, 0, 3, 4).astype(F32)).astype(BF16).reshape(4, 1, 128, 128)
    return (out, grad, filter_grad)


def solution(mesh):
    placed = (
        P("filt", "space", None, None),
        P("filt", "space"),
        P("filt", None, None),
        P("filt", "space", None, None),
    )
    return jax.shard_map(
        local,
        mesh=mesh,
        in_specs=placed,
        out_specs=(
            P("filt", "space", None, None),
            P("filt", "space", None, None),
            P("filt", None, None),
        ),
        check_vma=False,
    )
```

```python
import math

import jax
import jax.numpy as jnp
from jax import lax
from jax.experimental import pallas as pl
from jax.experimental.pallas import tpu as pltpu
from jax.sharding import PartitionSpec as P


F32 = jnp.float32
BF16 = jnp.bfloat16
PARAMS = pltpu.CompilerParams(vmem_limit_bytes=16 * 1024 * 1024)


def select_rows(rows, source, columns):
    row = lax.broadcasted_iota(jnp.int32, (rows, 128), 0)[:, :1]
    col = lax.broadcasted_iota(jnp.int32, (rows, columns), 1)
    return jnp.where(source(row) == col, 1.0, 0.0).astype(BF16)


def moved(matrix, cells):
    return jnp.dot(matrix, cells, preferred_element_type=F32).astype(BF16)


def by_24(n):
    part = (n * 2731) >> 16
    return part, n - part * 24


def by_32(n):
    return n >> 5, (n >> 1) & 15, n & 1


def pack_first(n):
    part, m = by_24(n)
    r, core = part >> 1, part & 1
    i, w = (m - 8) >> 3, m & 7
    rim = 64 + i * 64 + r * 4 + w + 14
    corner = 192 + (r & 3) * 4 + i * 2 + (w >> 2)
    inner = (w >= 1) & (w <= 6)
    return core * 208 + jnp.where(m < 8, (m >> 2) * 32 + r * 4 + (m & 3), jnp.where(inner, rim, corner))


def message_row(n):
    cell = (n & 15) * 24 + (n >> 6) * 4 + ((n >> 4) & 3)
    w, g, i = by_32(n - 128)
    rim = g * 24 + i * 8 + w + 9
    g, corner = (n - 320) >> 2, (n - 320) & 3
    return jnp.where(n < 128, cell, jnp.where(n < 320, rim, g * 24 + 8 + (corner >> 1) * 8 + (corner & 1) * 7))


def by_28(n):
    part = (n * 2341) >> 16
    return part, n - part * 28


def matrix_row(n):
    g, m = by_28(n)
    i, w = (m - 8) >> 3, m & 7
    cell = (m >> 2) * 64 + (m & 3) * 16 + g
    rim = 128 + (w - 1) * 32 + g * 2 + i
    rim = jnp.where((w >= 1) & (w <= 6), rim, 320 + g * 4 + i * 2 + (w >> 2))
    return jnp.where(m < 8, cell, jnp.where(m < 24, rim, 384 + g * 4 + m - 24))


def quarter_of(rank):
    return (rank >> 1) & 3


def own_rows(slab, weights_ref):
    lane = lax.broadcasted_iota(jnp.int32, (16, 128), 1) >> 5
    weights = jnp.concatenate([weights_ref[tap] for tap in range(27)], axis=0)
    result = []
    for core in range(2):
        source = lambda n: (slab >> 1) * 64 + ((n >> 1) & 15) * 4 + core * 2 + (n & 1)
        row = lax.broadcasted_iota(jnp.int32, (256, 128), 0)
        col = lax.broadcasted_iota(jnp.int32, (256, 128), 1)
        pick = jnp.where(source(col) == row, 1.0, 0.0).astype(BF16)
        picked = moved(weights, pick)
        rows = jnp.zeros((16, 128), F32)
        for tap in range(4):
            order = select_rows(16, lambda n: (4 * (n & 7) + tap) * 4 + (n >> 3) * 2 + (slab & 1), 108)
            rows = jnp.where(lane == tap, jnp.dot(order, picked, preferred_element_type=F32), rows)
        result.append(rows.astype(BF16))
    return result


def first_kernel(
    scales_ref, cells_ref, rims_ref, weights_ref, out_ref, scales, raw, cells, rims, weights, packed, sems
):
    copies = [
        pltpu.make_async_copy(cells_ref, raw, sems.at[0]),
        pltpu.make_async_copy(rims_ref, rims.at[:, 16:144], sems.at[1]),
        pltpu.make_async_copy(scales_ref, scales, sems.at[2]),
        pltpu.make_async_copy(weights_ref, weights, sems.at[3]),
    ]
    for copy in copies:
        copy.start()
    order = select_rows(384, pack_first, 416)
    for n in range(4):
        rims[n, :16] = jnp.zeros((16, 128), BF16)
        rims[n, 144:] = jnp.zeros((16, 128), BF16)
    for copy in copies:
        copy.wait()
    for n in range(4):
        cells[n] = (raw[n].astype(F32) * scales[:, n : n + 1]).astype(BF16)
    own = own_rows(lax.axis_index("space"), weights)
    for block in range(4):
        at = block * 32
        parts = []
        for core in range(2):
            parts += [cells[2 * core + i, at : at + 32] for i in range(2)]
            parts += [rims[2 * core + i, at : at + 64] for i in range(2)]
            parts.append(own[core])
        part = slice(block * 384, block * 384 + 384)
        packed[part] = moved(order, jnp.concatenate(parts, axis=0))
        copies.append(pltpu.make_async_copy(packed.at[part], out_ref.at[part], sems.at[4 + block]))
        copies[-1].start()
    for copy in copies[4:]:
        copy.wait()


def middle_kernel(got_ref, out_ref, corners_ref, cells, rims, sems):
    copies = []
    order = select_rows(128, message_row, 384)
    for block in range(4):
        rows = moved(order, got_ref[block * 384 : block * 384 + 384])
        for i in range(2):
            for y in range(4):
                piece = rows[i * 64 + y * 16 : i * 64 + y * 16 + 16]
                cells[i, y * 64 + block * 16 : y * 64 + block * 16 + 16] = piece
    for to in range(8):
        copies.append(pltpu.make_async_copy(cells.at[to % 2], out_ref.at[to, 0:256], sems.at[8 + to]))
        copies[-1].start()
    order = select_rows(256, lambda n: message_row(n + 128), 384)
    for block in range(4):
        rows = moved(order, got_ref[block * 384 : block * 384 + 384])
        rims[block] = rows[:192]
        for i in range(2):
            to = 2 * block + i
            copies.append(pltpu.make_async_copy(rims.at[block], out_ref.at[to, 256:448], sems.at[to]))
            copies[-1].start()
        corners_ref[block * 64 : block * 64 + 64] = rows[192:]
    for copy in copies:
        copy.wait()


def filter_kernel(rank_ref, own_ref, first_ref, second_ref, third_ref, filter_ref, stacked_ref, quarters):
    rank = rank_ref[0]
    for n, ref in enumerate((own_ref, first_ref, second_ref, third_ref)):
        quarters[quarter_of(rank) ^ n] = ref[...]
    by_n = select_rows(256, lambda n: (n & 63) * 4 + (n >> 6), 256)
    for h in range(2):
        for part in range(2):
            lanes = moved(by_n, quarters[2 * ((rank & 1) ^ part) + h])
            for n in range(4 - h):
                at = (4 * h + n) * 128
                filter_ref[part * 64 : part * 64 + 64, at : at + 128] = lanes[n * 64 : n * 64 + 64]
    same = select_rows(128, lambda n: n, 128)
    turned = [
        lax.dot_general(
            same,
            filter_ref[:, j * 128 : j * 128 + 128],
            (((1,), (1,)), ((), ())),
            preferred_element_type=F32,
        ).astype(BF16)
        for j in range(7)
    ]
    turned = jnp.concatenate(turned, axis=0)
    for a in range(3):
        stacked_ref[:, a * 128 : a * 128 + 128] = turned[a * 288 : a * 288 + 288]


def plane_of(mine_ref, theirs_ref, z):
    halves = [
        jnp.concatenate([ref[z, y * 64 : y * 64 + 64] for y in range(4)], axis=1) for ref in (mine_ref, theirs_ref)
    ]
    return jnp.concatenate(halves, axis=0)


def forward_kernel(mine_ref, theirs_ref, stacked_ref, out_ref, planes):
    planes[0] = jnp.zeros((128, 512), BF16)
    planes[9] = jnp.zeros((128, 512), BF16)
    for z in range(8):
        planes[z + 1] = plane_of(mine_ref, theirs_ref, z)
    column = lax.broadcasted_iota(jnp.int32, (32, 128), 1)

    def plane(z):
        near = jnp.concatenate([planes[z], planes[z + 1], planes[z + 2]], axis=0)
        terms = jnp.dot(stacked_ref[...], near, preferred_element_type=F32)
        for row in range(6):
            sums = []
            for e in range(3):
                total = None
                for b in range(3):
                    y = row + b - 2
                    if 0 <= y < 4:
                        at = b * 96 + e * 32
                        term = terms[at : at + 32, y * 128 : y * 128 + 128]
                        total = term if total is None else total + term
                sums.append(total)
            left = jnp.where(column >= 1, pltpu.roll(sums[0], 1, 1), 0.0)
            right = jnp.where(column <= 126, pltpu.roll(sums[2], 127, 1), 0.0)
            out_ref[z, row * 32 : row * 32 + 32] = (sums[1] + left + right).astype(BF16)

    for z in range(8):
        plane(z)


def fill_image(image, shifted, z):
    for a in range(3):
        for b in range(3):
            at = (a * 3 + b) * 96
            image[at : at + 96] = shifted[z + 2 - a, :, (2 - b) * 128 : (2 - b) * 128 + 512]


def shift(got_ref, shifted):
    before = select_rows(128, lambda n: n - 1, 128)
    after = select_rows(128, lambda n: n + 1, 128)
    shifted[0] = jnp.zeros((96, 768), BF16)
    shifted[9] = jnp.zeros((96, 768), BF16)

    for z in range(8):
        rows = got_ref[z, 256:448]
        for e, cells in ((0, moved(rows, before)), (1, rows), (2, moved(rows, after))):
            for y in range(6):
                shifted[z + 1, e * 32 : e * 32 + 32, y * 128 : y * 128 + 128] = cells[y * 32 : y * 32 + 32]


def backward_kernel(got_ref, filter_ref, keep_ref, send_ref, shifted, images):
    shift(got_ref, shifted)
    images[:, 864:896] = jnp.zeros((2, 32, 512), BF16)
    for z in range(8):
        image = images.at[z % 2]
        fill_image(image, shifted, z)
        grad = jnp.dot(filter_ref[...], image[...], preferred_element_type=F32)
        for y in range(4):
            keep_ref[z, y * 64 : y * 64 + 64] = grad[:64, y * 128 : y * 128 + 128]
            send_ref[z, y * 64 : y * 64 + 64] = grad[64:, y * 128 : y * 128 + 128].astype(BF16)


def sum_kernel(keep_ref, other_ref, rims_ref, out_ref, rows_ref, sems):
    copies = [pltpu.make_async_copy(rims_ref, out_ref.at[:, 256:448], sems.at[4])]
    copies[0].start()
    for n in range(4):
        part = slice(n * 2, n * 2 + 2)
        rows_ref[part] = (keep_ref[part] + other_ref[part].astype(F32)).astype(BF16)
        copies.append(pltpu.make_async_copy(rows_ref.at[part], out_ref.at[part, 0:256], sems.at[n]))
        copies[-1].start()
    for copy in copies:
        copy.wait()


def filter_grad_kernel(rank_ref, got_ref, theirs_ref, own_ref, send_ref, shifted, image, total):
    shift(got_ref, shifted)
    image[864:896] = jnp.zeros((32, 2048), BF16)
    total[...] = jnp.zeros((1024, 128), F32)
    for half in range(2):
        for z in range(4):
            fill_image(image.at[:, z * 512 : z * 512 + 512], shifted, half * 4 + z)
        cells = jnp.concatenate([plane_of(got_ref, theirs_ref, half * 4 + z) for z in range(4)], axis=1)
        total[:896] += lax.dot_general(image[...], cells, (((1,), (1,)), ((), ())), preferred_element_type=F32)
    rank = rank_ref[0]
    for n, ref in enumerate((own_ref, send_ref)):
        part = (((rank >> 1) ^ n ^ rank) & 1) * 64
        order = select_rows(256, lambda n: (n & 3) * 128 + part + (n >> 2), 512)
        for h in range(2):
            lanes = [total[j * 128 : j * 128 + 128].astype(BF16) for j in range(4 * h, 4 * h + 4)]
            ref[h * 256 : h * 256 + 256] = lax.dot_general(
                order, jnp.concatenate(lanes, axis=1), (((1,), (1,)), ((), ())), preferred_element_type=F32
            ).astype(BF16)


def last_kernel(got_ref, own_ref, other_ref, out_ref, grads):
    order = select_rows(448, matrix_row, 448)
    for i in range(2):
        grad = got_ref[i, :256].astype(F32)
        for n in range(1, 4):
            grad = grad + got_ref[2 * n + i, :256].astype(F32)
        grads[i] = grad.astype(BF16)
    for block in range(4):
        parts = []
        for i in range(2):
            parts += [grads[i, y * 64 + block * 16 : y * 64 + block * 16 + 16] for y in range(4)]
        rims = [got_ref[2 * block + i, 256:448].astype(F32) for i in range(2)]
        parts.append((rims[0] + rims[1]).astype(BF16))
        for h in range(2):
            part = slice(h * 256 + block * 64, h * 256 + block * 64 + 64)
            parts.append((own_ref[part].astype(F32) + other_ref[part].astype(F32)).astype(BF16))
        out_ref[block * 448 : block * 448 + 448] = moved(order, jnp.concatenate(parts, axis=0))


def tail_kernel(got_ref, out_ref):
    row = lax.broadcasted_iota(jnp.int32, (32, 1792), 0)
    col = lax.broadcasted_iota(jnp.int32, (32, 1792), 1)
    sender, m = by_28(col)
    corner = (m >= 8) & (((m & 7) == 0) | ((m & 7) == 7) | (m >= 24))
    n = jnp.where(m < 24, ((m - 8) >> 3) * 2 + ((m & 7) >> 2), m - 20)
    target = ((sender >> 1) & 1) * 16 + (sender & 1) * 8 + n
    order = jnp.where(corner & (target == row), 1.0, 0.0).astype(BF16)
    rows = jnp.dot(order, got_ref[...], preferred_element_type=F32)
    for n in range(8):
        out_ref[n] = rows


def finish_kernel(parts_ref, out_ref, by_tap):
    low = lax.broadcasted_iota(jnp.int32, (8, 128), 1) < 64
    norm = 1.0 / math.sqrt(131072)
    rows = []
    for c in range(2):
        for x in range(2):
            for y in range(4):
                rows.append(jnp.concatenate([parts_ref[2 * y + x, 2 * c + k] for k in range(2)], axis=1))
    rows = jnp.concatenate(rows, axis=0) * norm
    high = rows.astype(BF16)
    rest = rows - high.astype(F32)
    middle = rest.astype(BF16)
    low_bits = (rest - middle.astype(F32)).astype(BF16)
    row = lax.broadcasted_iota(jnp.int32, (256, 256), 0)
    lane = lax.broadcasted_iota(jnp.int32, (256, 256), 1)
    source = ((lane >> 1) & 1) * 128 + (lane >> 6) * 32 + ((lane >> 2) & 15) * 2 + (lane & 1)
    spread = jnp.where(source == row, 1.0, 0.0).astype(BF16)
    terms = jnp.dot(jnp.concatenate([high, middle, low_bits], axis=0), spread, preferred_element_type=F32)
    both = terms[:128] + (terms[128:256] + terms[256:])
    for pair in range(2):
        wide = both[:, pair * 128 : pair * 128 + 128]
        for channel in range(4):
            for half in range(2):
                at = (channel * 4 + half * 2) * 8
                even, odd = wide[at : at + 8], wide[at + 8 : at + 16]
                by_tap[channel * 2 + half, pl.ds(2 * pair, 8, stride=4)] = jnp.where(low, even, pltpu.roll(odd, 64, 1))
                by_tap[channel * 2 + half, pl.ds(2 * pair + 1, 8, stride=4)] = jnp.where(
                    low, pltpu.roll(even, 64, 1), odd
                )
    for channel in range(4):
        for half in range(2):
            out_ref[:, channel, half * 128 : half * 128 + 128] = by_tap[channel * 2 + half, :27]


def overlapped(parts):
    lead = parts.shape[:-3]
    keep = [(0, 0)] * len(lead)
    first = jnp.pad(parts[..., 1:4, :], keep + [(0, 1), (1, 0), (0, 0)])
    second = jnp.pad(parts[..., 4:7, :], keep + [(1, 0), (0, 1), (0, 0)])
    return (first + second).reshape(lead + (132, 128))[..., 2:130, :]


def whole(*shape):
    return pl.BlockSpec(shape, lambda n: (0,) * len(shape))


SCALAR = pl.BlockSpec(memory_space=pltpu.SMEM)
HBM = pl.BlockSpec(memory_space=pltpu.HBM)
DMA = pltpu.SemaphoreType.DMA


def call(kernel, name, ins, outs, scratch, flops, out_specs=None, mib=16):
    return pl.pallas_call(
        kernel,
        grid=(1,),
        in_specs=ins,
        out_shape=[jax.ShapeDtypeStruct(shape, dtype) for shape, dtype in outs],
        out_specs=out_specs or [whole(*shape) for shape, _ in outs],
        scratch_shapes=[pltpu.VMEM(*s) if isinstance(s, tuple) else s for s in scratch],
        compiler_params=pltpu.CompilerParams(vmem_limit_bytes=mib * 1024 * 1024),
        cost_estimate=pl.CostEstimate(flops=flops, bytes_accessed=4 << 20, transcendentals=0),
        name=name,
    )


def swapped(array, axis, bit):
    count = lax.axis_size(axis)
    return lax.ppermute(array, axis, [(n, n ^ bit) for n in range(count)])


def local(quantized, scales, weights, cotangent):
    rank = lax.axis_index("filt").reshape(1).astype(jnp.int32)

    (both,) = call(
        first_kernel,
        "first",
        [HBM] * 4,
        [((1536, 128), BF16)],
        [
            ((1, 4), F32),
            ((4, 128, 128), BF16),
            ((4, 128, 128), BF16),
            ((4, 160, 128), BF16),
            ((27, 4, 256), BF16),
            ((1536, 128), BF16),
            DMA((8,)),
        ],
        2 * 4 * 384 * 416 * 128,
        [HBM],
        mib=56,
    )(
        scales.reshape(1, 4),
        quantized.reshape(4, 128, 128),
        cotangent.reshape(4, 128, 128),
        weights.transpose(1, 0, 2),
    )
    got = lax.all_to_all(both.reshape(64, 24, 128), "filt", 0, 0, tiled=True)

    both, filters = call(
        middle_kernel,
        "middle",
        [whole(1536, 128)],
        [((8, 448, 128), BF16), ((256, 128), BF16)],
        [((2, 256, 128), BF16), ((4, 192, 128), BF16), DMA((16,))],
        2 * 4 * 384 * 384 * 128,
        [HBM, whole(256, 128)],
    )(got.reshape(1536, 128))
    got = lax.all_to_all(both, "space", 0, 0, tiled=True)
    filters = [filters] + [swapped(filters, "filt", 2 * n) for n in range(1, 4)]
    filters, stacked = call(
        filter_kernel,
        "filters",
        [SCALAR] + [whole(256, 128)] * 4,
        [((128, 896), BF16), ((288, 384), BF16)],
        [((4, 256, 128), BF16)],
        2 * 4 * 256 * 256 * 128,
    )(rank, *filters)

    filters, stacked, got = lax.optimization_barrier((filters, stacked, got))
    theirs = swapped(got[:, :256], "filt", 1)
    keep, send = call(
        backward_kernel,
        "backward",
        [whole(8, 448, 128), whole(128, 896)],
        [((8, 256, 128), F32), ((8, 256, 128), BF16)],
        [((10, 96, 768), BF16), ((2, 896, 512), BF16)],
        2 * 8 * 896 * 128 * 512,
    )(got, filters)
    other = swapped(send, "filt", 1)
    cells = pl.BlockSpec((8, 256, 128), lambda n: (0, 0, 0))
    (out,) = call(
        forward_kernel,
        "forward",
        [cells, whole(8, 256, 128), whole(288, 384)],
        [((8, 192, 128), BF16)],
        [((10, 128, 512), BF16)],
        2 * 8 * 288 * 384 * 512,
    )(got, theirs, stacked)
    (both,) = call(
        sum_kernel,
        "sum",
        [whole(8, 256, 128), whole(8, 256, 128), whole(8, 192, 128)],
        [((8, 448, 128), BF16)],
        [((8, 256, 128), BF16), DMA((5,))],
        8 * 256 * 128,
        [HBM],
    )(keep, other, out)
    both, cells, theirs = lax.optimization_barrier((both, got, theirs))

    terms = call(
        filter_grad_kernel,
        "filter_grad",
        [SCALAR, whole(8, 448, 128), whole(8, 256, 128)],
        [((512, 128), BF16)] * 2,
        [((10, 96, 768), BF16), ((896, 2048), BF16), ((1024, 128), F32)],
        2 * 8 * 896 * 128 * 512,
    )(rank, cells, theirs)

    got = lax.all_to_all(both, "space", 0, 0, tiled=True)
    (both,) = call(
        last_kernel,
        "last",
        [whole(8, 448, 128)] + [whole(512, 128)] * 2,
        [((1792, 128), BF16)],
        [((2, 256, 128), BF16)],
        2 * 4 * 384 * 384 * 128,
    )(got, terms[0], swapped(terms[1], "filt", 2))
    got = lax.all_to_all(both.reshape(448, 4, 128), "filt", 0, 0, tiled=True)

    (terms,) = call(
        tail_kernel, "tail", [whole(1792, 128)], [((8, 32, 128), F32)], [], 2 * 32 * 1792 * 128
    )(got.reshape(1792, 128))
    terms, got = lax.optimization_barrier((terms, got.reshape(32, 2, 28, 128)))
    terms = lax.all_to_all(terms, "space", 0, 0, tiled=True).reshape(8, 4, 8, 128)
    filter_grad = pl.pallas_call(
        finish_kernel,
        out_shape=jax.ShapeDtypeStruct((27, 4, 256), F32),
        scratch_shapes=[pltpu.VMEM((8, 32, 128), F32)],
        compiler_params=PARAMS,
        name="finish",
    )(terms).transpose(1, 0, 2)

    grad = got[:, :, :8].reshape(32, 2, 2, 4, 128).transpose(1, 2, 0, 3, 4).reshape(4, 1, 128, 128)
    rims = got[:, :, 8:24].reshape(32, 2, 2, 8, 128)
    out = overlapped(rims.transpose(1, 2, 0, 3, 4).astype(F32)).astype(BF16).reshape(4, 1, 128, 128)
    return (out, grad, filter_grad)


def solution(mesh):
    placed = (
        P("filt", "space", None, None),
        P("filt", "space"),
        P("filt", None, None),
        P("filt", "space", None, None),
    )
    return jax.shard_map(
        local,
        mesh=mesh,
        in_specs=placed,
        out_specs=(
            P("filt", "space", None, None),
            P("filt", "space", None, None),
            P("filt", None, None),
        ),
        check_vma=False,
    )
```

```python
import math

import jax
import jax.numpy as jnp
from jax import lax
from jax.experimental import pallas as pl
from jax.experimental.pallas import tpu as pltpu
from jax.sharding import PartitionSpec as P


F32 = jnp.float32
BF16 = jnp.bfloat16
PARAMS = pltpu.CompilerParams(vmem_limit_bytes=16 * 1024 * 1024)


def select_rows(rows, source, columns):
    row = lax.broadcasted_iota(jnp.int32, (rows, 128), 0)[:, :1]
    col = lax.broadcasted_iota(jnp.int32, (rows, columns), 1)
    return jnp.where(source(row) == col, 1.0, 0.0).astype(BF16)


def moved(matrix, cells):
    return jnp.dot(matrix, cells, preferred_element_type=F32).astype(BF16)


def by_24(n):
    part = (n * 2731) >> 16
    return part, n - part * 24


def by_32(n):
    return n >> 5, (n >> 1) & 15, n & 1


def pack_first(n):
    part, m = by_24(n)
    r, core = part >> 1, part & 1
    i, w = (m - 8) >> 3, m & 7
    rim = 64 + i * 64 + r * 4 + w + 14
    corner = 192 + (r & 3) * 4 + i * 2 + (w >> 2)
    inner = (w >= 1) & (w <= 6)
    return core * 208 + jnp.where(m < 8, (m >> 2) * 32 + r * 4 + (m & 3), jnp.where(inner, rim, corner))


def message_row(n):
    cell = (n & 15) * 24 + (n >> 6) * 4 + ((n >> 4) & 3)
    w, g, i = by_32(n - 128)
    rim = g * 24 + i * 8 + w + 9
    g, corner = (n - 320) >> 2, (n - 320) & 3
    return jnp.where(n < 128, cell, jnp.where(n < 320, rim, g * 24 + 8 + (corner >> 1) * 8 + (corner & 1) * 7))


def by_28(n):
    part = (n * 2341) >> 16
    return part, n - part * 28


def matrix_row(n):
    g, m = by_28(n)
    i, w = (m - 8) >> 3, m & 7
    cell = (m >> 2) * 64 + (m & 3) * 16 + g
    rim = 128 + (w - 1) * 32 + g * 2 + i
    rim = jnp.where((w >= 1) & (w <= 6), rim, 320 + g * 4 + i * 2 + (w >> 2))
    return jnp.where(m < 8, cell, jnp.where(m < 24, rim, 384 + g * 4 + m - 24))


def quarter_of(rank):
    return (rank >> 1) & 3


def own_rows(slab, weights_ref):
    lane = lax.broadcasted_iota(jnp.int32, (16, 128), 1) >> 5
    weights = jnp.concatenate([weights_ref[tap] for tap in range(27)], axis=0)
    result = []
    for core in range(2):
        source = lambda n: (slab >> 1) * 64 + ((n >> 1) & 15) * 4 + core * 2 + (n & 1)
        row = lax.broadcasted_iota(jnp.int32, (256, 128), 0)
        col = lax.broadcasted_iota(jnp.int32, (256, 128), 1)
        pick = jnp.where(source(col) == row, 1.0, 0.0).astype(BF16)
        picked = moved(weights, pick)
        rows = jnp.zeros((16, 128), F32)
        for tap in range(4):
            order = select_rows(16, lambda n: (4 * (n & 7) + tap) * 4 + (n >> 3) * 2 + (slab & 1), 108)
            rows = jnp.where(lane == tap, jnp.dot(order, picked, preferred_element_type=F32), rows)
        result.append(rows.astype(BF16))
    return result


def first_kernel(
    scales_ref, cells_ref, rims_ref, weights_ref, out_ref, scales, raw, cells, rims, weights, packed, sems
):
    copies = [
        pltpu.make_async_copy(cells_ref, raw, sems.at[0]),
        pltpu.make_async_copy(rims_ref, rims.at[:, 16:144], sems.at[1]),
        pltpu.make_async_copy(scales_ref, scales, sems.at[2]),
        pltpu.make_async_copy(weights_ref, weights, sems.at[3]),
    ]
    for copy in copies:
        copy.start()
    order = select_rows(384, pack_first, 416)
    for n in range(4):
        rims[n, :16] = jnp.zeros((16, 128), BF16)
        rims[n, 144:] = jnp.zeros((16, 128), BF16)
    for copy in copies:
        copy.wait()
    for n in range(4):
        cells[n] = (raw[n].astype(F32) * scales[:, n : n + 1]).astype(BF16)
    own = own_rows(lax.axis_index("space"), weights)
    for block in range(4):
        at = block * 32
        parts = []
        for core in range(2):
            parts += [cells[2 * core + i, at : at + 32] for i in range(2)]
            parts += [rims[2 * core + i, at : at + 64] for i in range(2)]
            parts.append(own[core])
        part = slice(block * 384, block * 384 + 384)
        packed[part] = moved(order, jnp.concatenate(parts, axis=0))
        copies.append(pltpu.make_async_copy(packed.at[part], out_ref.at[part], sems.at[4 + block]))
        copies[-1].start()
    for copy in copies[4:]:
        copy.wait()


def middle_kernel(got_ref, out_ref, corners_ref, cells, rims, sems):
    copies = []
    order = select_rows(128, message_row, 384)
    for block in range(4):
        rows = moved(order, got_ref[block * 384 : block * 384 + 384])
        for i in range(2):
            for y in range(4):
                piece = rows[i * 64 + y * 16 : i * 64 + y * 16 + 16]
                cells[i, y * 64 + block * 16 : y * 64 + block * 16 + 16] = piece
    for to in range(8):
        copies.append(pltpu.make_async_copy(cells.at[to % 2], out_ref.at[to, 0:256], sems.at[8 + to]))
        copies[-1].start()
    order = select_rows(256, lambda n: message_row(n + 128), 384)
    for block in range(4):
        rows = moved(order, got_ref[block * 384 : block * 384 + 384])
        rims[block] = rows[:192]
        for i in range(2):
            to = 2 * block + i
            copies.append(pltpu.make_async_copy(rims.at[block], out_ref.at[to, 256:448], sems.at[to]))
            copies[-1].start()
        corners_ref[block * 64 : block * 64 + 64] = rows[192:]
    for copy in copies:
        copy.wait()


def filter_kernel(rank_ref, own_ref, first_ref, second_ref, third_ref, filter_ref, stacked_ref, quarters):
    rank = rank_ref[0]
    for n, ref in enumerate((own_ref, first_ref, second_ref, third_ref)):
        quarters[quarter_of(rank) ^ n] = ref[...]
    by_n = select_rows(256, lambda n: (n & 63) * 4 + (n >> 6), 256)
    for h in range(2):
        for part in range(2):
            lanes = moved(by_n, quarters[2 * ((rank & 1) ^ part) + h])
            for n in range(4 - h):
                at = (4 * h + n) * 128
                filter_ref[part * 64 : part * 64 + 64, at : at + 128] = lanes[n * 64 : n * 64 + 64]
    same = select_rows(128, lambda n: n, 128)
    turned = [
        lax.dot_general(
            same,
            filter_ref[:, j * 128 : j * 128 + 128],
            (((1,), (1,)), ((), ())),
            preferred_element_type=F32,
        ).astype(BF16)
        for j in range(7)
    ]
    turned = jnp.concatenate(turned, axis=0)
    for a in range(3):
        stacked_ref[:, a * 128 : a * 128 + 128] = turned[a * 288 : a * 288 + 288]


def plane_of(mine_ref, theirs_ref, z):
    halves = [
        jnp.concatenate([ref[z, y * 64 : y * 64 + 64] for y in range(4)], axis=1) for ref in (mine_ref, theirs_ref)
    ]
    return jnp.concatenate(halves, axis=0)


def forward_kernel(mine_ref, theirs_ref, stacked_ref, out_ref, planes):
    for z in range(8):
        planes[z + 1] = plane_of(mine_ref, theirs_ref, z)
    column = lax.broadcasted_iota(jnp.int32, (32, 128), 1)

    def plane(z):
        taps = range(1 if z == 0 else 0, 2 if z == 7 else 3)
        near = jnp.concatenate([planes[z + tap] for tap in taps], axis=0)
        used = stacked_ref[:, taps[0] * 128 : taps[-1] * 128 + 128]
        terms = jnp.dot(used, near, preferred_element_type=F32)
        for row in range(6):
            sums = []
            for e in range(3):
                total = None
                for b in range(3):
                    y = row + b - 2
                    if 0 <= y < 4:
                        at = b * 96 + e * 32
                        term = terms[at : at + 32, y * 128 : y * 128 + 128]
                        total = term if total is None else total + term
                sums.append(total)
            left = jnp.where(column >= 1, pltpu.roll(sums[0], 1, 1), 0.0)
            right = jnp.where(column <= 126, pltpu.roll(sums[2], 127, 1), 0.0)
            out_ref[z, row * 32 : row * 32 + 32] = (sums[1] + left + right).astype(BF16)

    for z in range(8):
        plane(z)


def fill_image(image, shifted, z):
    for a in range(3):
        for b in range(3):
            at = (a * 3 + b) * 96
            image[at : at + 96] = shifted[z + 2 - a, :, (2 - b) * 128 : (2 - b) * 128 + 512]


def shift(got_ref, shifted):
    before = select_rows(128, lambda n: n - 1, 128)
    after = select_rows(128, lambda n: n + 1, 128)
    shifted[0] = jnp.zeros((96, 768), BF16)
    shifted[9] = jnp.zeros((96, 768), BF16)

    for z in range(8):
        rows = got_ref[z, 256:448]
        for e, cells in ((0, moved(rows, before)), (1, rows), (2, moved(rows, after))):
            for y in range(6):
                shifted[z + 1, e * 32 : e * 32 + 32, y * 128 : y * 128 + 128] = cells[y * 32 : y * 32 + 32]


def backward_kernel(got_ref, filter_ref, keep_ref, send_ref, shifted, images):
    shift(got_ref, shifted)
    images[:, 864:896] = jnp.zeros((2, 32, 512), BF16)
    for z in range(8):
        image = images.at[z % 2]
        fill_image(image, shifted, z)
        grad = jnp.dot(filter_ref[...], image[...], preferred_element_type=F32)
        for y in range(4):
            keep_ref[z, y * 64 : y * 64 + 64] = grad[:64, y * 128 : y * 128 + 128]
            send_ref[z, y * 64 : y * 64 + 64] = grad[64:, y * 128 : y * 128 + 128].astype(BF16)


def sum_kernel(keep_ref, other_ref, rims_ref, out_ref, rows_ref, sems):
    copies = [pltpu.make_async_copy(rims_ref, out_ref.at[:, 256:448], sems.at[4])]
    copies[0].start()
    for n in range(4):
        part = slice(n * 2, n * 2 + 2)
        rows_ref[part] = (keep_ref[part] + other_ref[part].astype(F32)).astype(BF16)
        copies.append(pltpu.make_async_copy(rows_ref.at[part], out_ref.at[part, 0:256], sems.at[n]))
        copies[-1].start()
    for copy in copies:
        copy.wait()


def filter_grad_kernel(rank_ref, got_ref, theirs_ref, own_ref, send_ref, shifted, image, total):
    shift(got_ref, shifted)
    image[864:896] = jnp.zeros((32, 2048), BF16)
    total[...] = jnp.zeros((1024, 128), F32)
    for half in range(2):
        for z in range(4):
            fill_image(image.at[:, z * 512 : z * 512 + 512], shifted, half * 4 + z)
        cells = jnp.concatenate([plane_of(got_ref, theirs_ref, half * 4 + z) for z in range(4)], axis=1)
        total[:896] += lax.dot_general(image[...], cells, (((1,), (1,)), ((), ())), preferred_element_type=F32)
    rank = rank_ref[0]
    for n, ref in enumerate((own_ref, send_ref)):
        part = (((rank >> 1) ^ n ^ rank) & 1) * 64
        order = select_rows(256, lambda n: (n & 3) * 128 + part + (n >> 2), 512)
        for h in range(2):
            lanes = [total[j * 128 : j * 128 + 128].astype(BF16) for j in range(4 * h, 4 * h + 4)]
            ref[h * 256 : h * 256 + 256] = lax.dot_general(
                order, jnp.concatenate(lanes, axis=1), (((1,), (1,)), ((), ())), preferred_element_type=F32
            ).astype(BF16)


def last_kernel(got_ref, own_ref, other_ref, out_ref, grads):
    order = select_rows(448, matrix_row, 448)
    for i in range(2):
        grad = got_ref[i, :256].astype(F32)
        for n in range(1, 4):
            grad = grad + got_ref[2 * n + i, :256].astype(F32)
        grads[i] = grad.astype(BF16)
    for block in range(4):
        parts = []
        for i in range(2):
            parts += [grads[i, y * 64 + block * 16 : y * 64 + block * 16 + 16] for y in range(4)]
        rims = [got_ref[2 * block + i, 256:448].astype(F32) for i in range(2)]
        parts.append((rims[0] + rims[1]).astype(BF16))
        for h in range(2):
            part = slice(h * 256 + block * 64, h * 256 + block * 64 + 64)
            parts.append((own_ref[part].astype(F32) + other_ref[part].astype(F32)).astype(BF16))
        out_ref[block * 448 : block * 448 + 448] = moved(order, jnp.concatenate(parts, axis=0))


def tail_kernel(got_ref, out_ref):
    row = lax.broadcasted_iota(jnp.int32, (32, 1792), 0)
    col = lax.broadcasted_iota(jnp.int32, (32, 1792), 1)
    sender, m = by_28(col)
    corner = (m >= 8) & (((m & 7) == 0) | ((m & 7) == 7) | (m >= 24))
    n = jnp.where(m < 24, ((m - 8) >> 3) * 2 + ((m & 7) >> 2), m - 20)
    target = ((sender >> 1) & 1) * 16 + (sender & 1) * 8 + n
    order = jnp.where(corner & (target == row), 1.0, 0.0).astype(BF16)
    rows = jnp.dot(order, got_ref[...], preferred_element_type=F32)
    for n in range(8):
        out_ref[n] = rows


def finish_kernel(parts_ref, out_ref, by_tap):
    low = lax.broadcasted_iota(jnp.int32, (8, 128), 1) < 64
    norm = 1.0 / math.sqrt(131072)
    rows = []
    for c in range(2):
        for x in range(2):
            for y in range(4):
                rows.append(jnp.concatenate([parts_ref[2 * y + x, 2 * c + k] for k in range(2)], axis=1))
    rows = jnp.concatenate(rows, axis=0) * norm
    high = rows.astype(BF16)
    rest = rows - high.astype(F32)
    middle = rest.astype(BF16)
    low_bits = (rest - middle.astype(F32)).astype(BF16)
    row = lax.broadcasted_iota(jnp.int32, (256, 256), 0)
    lane = lax.broadcasted_iota(jnp.int32, (256, 256), 1)
    source = ((lane >> 1) & 1) * 128 + (lane >> 6) * 32 + ((lane >> 2) & 15) * 2 + (lane & 1)
    spread = jnp.where(source == row, 1.0, 0.0).astype(BF16)
    terms = jnp.dot(jnp.concatenate([high, middle, low_bits], axis=0), spread, preferred_element_type=F32)
    both = terms[:128] + (terms[128:256] + terms[256:])
    for pair in range(2):
        wide = both[:, pair * 128 : pair * 128 + 128]
        for channel in range(4):
            for half in range(2):
                at = (channel * 4 + half * 2) * 8
                even, odd = wide[at : at + 8], wide[at + 8 : at + 16]
                by_tap[channel * 2 + half, pl.ds(2 * pair, 8, stride=4)] = jnp.where(low, even, pltpu.roll(odd, 64, 1))
                by_tap[channel * 2 + half, pl.ds(2 * pair + 1, 8, stride=4)] = jnp.where(
                    low, pltpu.roll(even, 64, 1), odd
                )
    for channel in range(4):
        for half in range(2):
            out_ref[:, channel, half * 128 : half * 128 + 128] = by_tap[channel * 2 + half, :27]


def overlapped(parts):
    lead = parts.shape[:-3]
    keep = [(0, 0)] * len(lead)
    first = jnp.pad(parts[..., 1:4, :], keep + [(0, 1), (1, 0), (0, 0)])
    second = jnp.pad(parts[..., 4:7, :], keep + [(1, 0), (0, 1), (0, 0)])
    return (first + second).reshape(lead + (132, 128))[..., 2:130, :]


def whole(*shape):
    return pl.BlockSpec(shape, lambda n: (0,) * len(shape))


SCALAR = pl.BlockSpec(memory_space=pltpu.SMEM)
HBM = pl.BlockSpec(memory_space=pltpu.HBM)
DMA = pltpu.SemaphoreType.DMA


def call(kernel, name, ins, outs, scratch, flops, out_specs=None, mib=16):
    return pl.pallas_call(
        kernel,
        grid=(1,),
        in_specs=ins,
        out_shape=[jax.ShapeDtypeStruct(shape, dtype) for shape, dtype in outs],
        out_specs=out_specs or [whole(*shape) for shape, _ in outs],
        scratch_shapes=[pltpu.VMEM(*s) if isinstance(s, tuple) else s for s in scratch],
        compiler_params=pltpu.CompilerParams(vmem_limit_bytes=mib * 1024 * 1024),
        cost_estimate=pl.CostEstimate(flops=flops, bytes_accessed=4 << 20, transcendentals=0),
        name=name,
    )


def swapped(array, axis, bit):
    count = lax.axis_size(axis)
    return lax.ppermute(array, axis, [(n, n ^ bit) for n in range(count)])


def local(quantized, scales, weights, cotangent):
    rank = lax.axis_index("filt").reshape(1).astype(jnp.int32)

    (both,) = call(
        first_kernel,
        "first",
        [HBM] * 4,
        [((1536, 128), BF16)],
        [
            ((1, 4), F32),
            ((4, 128, 128), BF16),
            ((4, 128, 128), BF16),
            ((4, 160, 128), BF16),
            ((27, 4, 256), BF16),
            ((1536, 128), BF16),
            DMA((8,)),
        ],
        2 * 4 * 384 * 416 * 128,
        [HBM],
        mib=56,
    )(
        scales.reshape(1, 4),
        quantized.reshape(4, 128, 128),
        cotangent.reshape(4, 128, 128),
        weights.transpose(1, 0, 2),
    )
    got = lax.all_to_all(both.reshape(64, 24, 128), "filt", 0, 0, tiled=True)

    both, filters = call(
        middle_kernel,
        "middle",
        [whole(1536, 128)],
        [((8, 448, 128), BF16), ((256, 128), BF16)],
        [((2, 256, 128), BF16), ((4, 192, 128), BF16), DMA((16,))],
        2 * 4 * 384 * 384 * 128,
        [HBM, whole(256, 128)],
    )(got.reshape(1536, 128))
    got = lax.all_to_all(both, "space", 0, 0, tiled=True)
    filters = [filters] + [swapped(filters, "filt", 2 * n) for n in range(1, 4)]
    filters, stacked = call(
        filter_kernel,
        "filters",
        [SCALAR] + [whole(256, 128)] * 4,
        [((128, 896), BF16), ((288, 384), BF16)],
        [((4, 256, 128), BF16)],
        2 * 4 * 256 * 256 * 128,
    )(rank, *filters)

    filters, stacked, got = lax.optimization_barrier((filters, stacked, got))
    theirs = swapped(got[:, :256], "filt", 1)
    keep, send = call(
        backward_kernel,
        "backward",
        [whole(8, 448, 128), whole(128, 896)],
        [((8, 256, 128), F32), ((8, 256, 128), BF16)],
        [((10, 96, 768), BF16), ((2, 896, 512), BF16)],
        2 * 8 * 896 * 128 * 512,
    )(got, filters)
    other = swapped(send, "filt", 1)
    cells = pl.BlockSpec((8, 256, 128), lambda n: (0, 0, 0))
    (out,) = call(
        forward_kernel,
        "forward",
        [cells, whole(8, 256, 128), whole(288, 384)],
        [((8, 192, 128), BF16)],
        [((10, 128, 512), BF16)],
        2 * 8 * 288 * 384 * 512,
    )(got, theirs, stacked)
    (both,) = call(
        sum_kernel,
        "sum",
        [whole(8, 256, 128), whole(8, 256, 128), whole(8, 192, 128)],
        [((8, 448, 128), BF16)],
        [((8, 256, 128), BF16), DMA((5,))],
        8 * 256 * 128,
        [HBM],
    )(keep, other, out)
    both, cells, theirs = lax.optimization_barrier((both, got, theirs))

    terms = call(
        filter_grad_kernel,
        "filter_grad",
        [SCALAR, whole(8, 448, 128), whole(8, 256, 128)],
        [((512, 128), BF16)] * 2,
        [((10, 96, 768), BF16), ((896, 2048), BF16), ((1024, 128), F32)],
        2 * 8 * 896 * 128 * 512,
    )(rank, cells, theirs)

    got = lax.all_to_all(both, "space", 0, 0, tiled=True)
    (both,) = call(
        last_kernel,
        "last",
        [whole(8, 448, 128)] + [whole(512, 128)] * 2,
        [((1792, 128), BF16)],
        [((2, 256, 128), BF16)],
        2 * 4 * 384 * 384 * 128,
    )(got, terms[0], swapped(terms[1], "filt", 2))
    got = lax.all_to_all(both.reshape(448, 4, 128), "filt", 0, 0, tiled=True)

    (terms,) = call(
        tail_kernel, "tail", [whole(1792, 128)], [((8, 32, 128), F32)], [], 2 * 32 * 1792 * 128
    )(got.reshape(1792, 128))
    terms, got = lax.optimization_barrier((terms, got.reshape(32, 2, 28, 128)))
    terms = lax.all_to_all(terms, "space", 0, 0, tiled=True).reshape(8, 4, 8, 128)
    filter_grad = pl.pallas_call(
        finish_kernel,
        out_shape=jax.ShapeDtypeStruct((27, 4, 256), F32),
        scratch_shapes=[pltpu.VMEM((8, 32, 128), F32)],
        compiler_params=PARAMS,
        name="finish",
    )(terms).transpose(1, 0, 2)

    grad = got[:, :, :8].reshape(32, 2, 2, 4, 128).transpose(1, 2, 0, 3, 4).reshape(4, 1, 128, 128)
    rims = got[:, :, 8:24].reshape(32, 2, 2, 8, 128)
    out = overlapped(rims.transpose(1, 2, 0, 3, 4).astype(F32)).astype(BF16).reshape(4, 1, 128, 128)
    return (out, grad, filter_grad)


def solution(mesh):
    placed = (
        P("filt", "space", None, None),
        P("filt", "space"),
        P("filt", None, None),
        P("filt", "space", None, None),
    )
    return jax.shard_map(
        local,
        mesh=mesh,
        in_specs=placed,
        out_specs=(
            P("filt", "space", None, None),
            P("filt", "space", None, None),
            P("filt", None, None),
        ),
        check_vma=False,
    )
```
